32 devices in a mesh: group: 2 (over y), expert: 16 (over z, x, core), tensor: 1.
Axes of the slice: x: 2, y: 2, z: 4, core: 2. Of those that a mesh axis runs over, the one named last changes fastest.
Arguments:
- tokens: bfloat16 [512, 2048], P(('group', 'expert')), parts along dimension 0, may hold values from -6 to 6
- route_weight: float32 [512, 8], P(('group', 'expert')), parts along dimension 0, may hold values from 0.02 to 1
- replica: int32 [512, 8], P(('group', 'expert')), parts along dimension 0, may hold values from 0 to 15, all different within a row; in each aligned block of 16 rows (0 to 15, 16 to 31, ...) at most 16 rows name the same one
- w_gate: bfloat16 [16, 2048, 768], P('expert', None, 'tensor'), may hold values from -0.125 to 0.125
- w_up: bfloat16 [16, 2048, 768], P('expert', None, 'tensor'), may hold values from -0.125 to 0.125
- w_down: bfloat16 [16, 768, 2048], P('expert', None, 'tensor'), may hold values from -0.21875 to 0.21875
Outputs:
- mixed: bfloat16 [512, 2048], P(('group', 'expert'), 'tensor'), parts along dimension 0
The draws below stay inside these ranges and needn't reach their ends.
There are 2 independent parts, one for each index of `group`. The reference program is written for one: setup_inputs(seed, part) draws one part's arguments, and reference() takes and returns one part's arrays. A program takes and returns all parts, laid end to end along the dimension named above; an argument that names none is the same for every part. Nothing has to cross between parts.
Inputs may be any that keep to these rules, and one draw needn't show every extreme that they name: Each row names 8 different replicas. Among the rows of one index of expert (aligned blocks of 16 rows) no replica is named more than 16 times, a bound that some block reaches.
All inputs are finite; a program needn't handle non-finite values.
Results may differ from the reference program's by a relative error of at most 0.0037.
Values may be sent and summed in bfloat16 or wider, within the bound.
No kernel may reach another device: no remote copies, remote signals or barrier semaphores. Data moves between devices by JAX's collectives and lax.ppermute only.
A program may use at most 64 MiB of HBM per device.

```python
import math
import jax
import jax.numpy as jnp
import numpy as np
from jax import lax

D = 2048
TOP = 8
FF_W = 768
TOK_DEV = 16
TOKENS = 256
SLOTS = 16
CAP = 16
N_EXPERT = 16


def shard_levels(own_key, extent, shards, least, top_value):
    loudness, own = 1.0, jax.random.fold_in(own_key, 6)
    for dim, shards_of in shards:
        steps = jnp.exp(jax.random.uniform(jax.random.fold_in(own, dim), (shards_of,), jnp.float32, least / len(shards), top_value / len(shards)))
        loudness = loudness * jnp.repeat(steps, extent[dim] // shards_of).reshape([-1 if axis == dim else 1 for axis in range(len(extent))])
    return loudness


def routed_block(stream_key, own, number, rows, number_of, top, most, skew):
    order = jax.random.permutation(stream_key, number_of)
    heavy_load, ordinary = shares(number_of, rows * top, most, skew, True), shares(number_of, rows * top, most, skew, False)
    places = jnp.arange(number_of)

    def named(sizes, turn):
        used = int((sizes > 0).sum())
        fixed = max(1, used // 4)
        moved = fixed + (places - fixed + turn * (used - fixed)) % max(1, number_of - fixed)
        return jnp.zeros((number_of,), jnp.int32).at[order[jnp.where(places < fixed, places, moved)]].set(jnp.asarray(sizes, jnp.int32))

    sizes = jnp.where(number % 4 == 0, named(heavy_load, number // 4), named(ordinary, number - number // 4 - 1))
    mixed = jax.random.permutation(jax.random.fold_in(own, 3), number_of)
    giver, receiver = mixed[0:number_of // 2 * 2:2], mixed[1:number_of // 2 * 2:2]
    margin = jnp.minimum(sizes[giver] - 1, most - sizes[receiver]) // 2
    margin = jnp.where((giver == order[0]) | (receiver == order[0]) | (sizes[receiver] == 0), 0, jnp.maximum(margin, 0))
    moved = jax.random.randint(jax.random.fold_in(own, 4), (number_of // 2,), 0, 1 << 20) % (margin + 1)
    sizes = sizes.at[giver].add(-moved).at[receiver].add(moved)
    items = jnp.searchsorted(jnp.cumsum(sizes), jnp.arange(rows * top), side="right").astype(jnp.int32)
    grid = items.reshape(top, rows).T
    grid = grid[jax.random.permutation(jax.random.fold_in(own, 1), rows)]
    turn = jax.random.randint(jax.random.fold_in(own, 2), (rows, 1), 0, top)
    return jnp.take_along_axis(grid, (jnp.arange(top)[None, :] + turn) % top, axis=1)


def shares(number_of, total, most, slope, full):
    loads = [(1 << 20) // math.isqrt(rank ** slope) + 1 for rank in range(1, number_of + 1)]
    largest = most if full else min(most, max(-(-total // number_of), total * loads[0] // sum(loads)))
    least = 1 if total - largest >= number_of - 1 else 0
    given, rest = [largest] + [least] * (number_of - 1), total - largest - least * (number_of - 1)
    while rest > 0:
        movable = [i for i in range(1, number_of) if given[i] < largest] or [i for i in range(1, number_of) if given[i] < most]
        whole, budget = sum([loads[i] for i in movable]), rest
        for i in movable:
            addition = min(most - given[i], max(1, budget * loads[i] // whole), rest)
            given[i] = given[i] + addition
            rest = rest - addition
    return np.array(given)


def normal_values(stream_key, shape, width, bound, pieces=(), kind=jnp.bfloat16):
    values = width * jax.random.normal(stream_key, shape, jnp.float32)
    if pieces:
        values = values * shard_levels(stream_key, shape, pieces, -0.22, 0.18)
    return jnp.clip(values, -bound, bound).astype(kind)


def setup_inputs(seed: int = 0, part: int = 0) -> dict:
    seeds = jax.random.split(jax.random.key(seed), 7)
    part_splits = jax.random.split(jax.random.fold_in(seeds[6], part), 7)
    tokens = normal_values(part_splits[0], (TOKENS, D), 1.0, 6.0, ((0, 16),))
    route_weight = jnp.clip(jnp.exp(math.log(1.0) - 3.912023 * jax.random.uniform(part_splits[1], (TOKENS, TOP), jnp.float32) ** shard_levels(part_splits[1], (TOKENS, TOP), ((0, 16),), -0.2, 0.2)), 0.02, 1.0)
    replica_keys = jax.random.split(jax.random.fold_in(part_splits[2], 1), TOKENS // TOK_DEV)
    replica_turns = jax.random.permutation(jax.random.fold_in(part_splits[2], 3), TOKENS // TOK_DEV)
    replica = jax.vmap(lambda own, number: routed_block(jax.random.fold_in(part_splits[2], 2), own, number, TOK_DEV, SLOTS, TOP, CAP, 2))(replica_keys, replica_turns).reshape((TOKENS, TOP))
    w_gate = normal_values(seeds[3], (SLOTS, D, FF_W), D ** -0.5, 0.125, ((0, 16),))
    w_up = normal_values(seeds[4], (SLOTS, D, FF_W), D ** -0.5, 0.125, ((0, 16),))
    w_down = normal_values(seeds[5], (SLOTS, FF_W, D), FF_W ** -0.5, 0.21875, ((0, 16),))
    return {"tokens": tokens, "route_weight": route_weight, "replica": replica, "w_gate": w_gate, "w_up": w_up, "w_down": w_down}


def reference(tokens, route_weight, replica, w_gate, w_up, w_down):
    prob = route_weight / jnp.sum(route_weight, axis=1, keepdims=True)
    limit = min(TOKENS, N_EXPERT * CAP)

    def one_slot(total, slot_id):
        chosen_mask = replica == slot_id
        share = jnp.sum(jnp.where(chosen_mask, prob, 0.0), axis=1)
        chosen = jnp.any(chosen_mask, axis=1)
        chosen_count = jnp.sum(chosen.astype(jnp.int32))
        row_ids = jnp.nonzero(chosen, size=limit, fill_value=0)[0].astype(jnp.int32)
        picked = tokens[row_ids]
        gate = jnp.dot(picked, w_gate[slot_id], preferred_element_type=jnp.float32)
        upward = jnp.dot(picked, w_up[slot_id], preferred_element_type=jnp.float32)
        hidden = (jax.nn.silu(gate) * upward).astype(jnp.bfloat16)
        result = jnp.dot(hidden, w_down[slot_id], preferred_element_type=jnp.float32).astype(jnp.bfloat16)
        result = lax.optimization_barrier(result).astype(jnp.float32)
        live = (jnp.arange(limit, dtype=jnp.int32) < chosen_count).astype(jnp.float32)
        term = result * (share[row_ids] * live)[:, None]
        return total.at[row_ids].add(term), None

    start = jnp.zeros((TOKENS, D), jnp.float32)
    total, unused = lax.scan(one_slot, start, jnp.arange(SLOTS, dtype=jnp.int32))
    return (tokens.astype(jnp.float32) + total).astype(jnp.bfloat16)
```

```python
import functools
import jax
import jax.numpy as jnp
from jax import lax
from jax.experimental import pallas as pl
from jax.experimental.pallas import tpu as pltpu
from jax.sharding import PartitionSpec as P

LANES = 128
VMEM = pl.BlockSpec(memory_space=pltpu.VMEM)
SMEM = pl.BlockSpec(memory_space=pltpu.SMEM)


def in_vmem(array):
    return pltpu.with_memory_space_constraint(array, pltpu.VMEM)


def pack_kernel(token_ref, weight_ref, replica_ref, out_ref):
    width = token_ref.shape[1]
    weight = weight_ref[...]
    probability = weight / jnp.sum(weight, axis=0, keepdims=True)
    top_count, row_count = weight.shape
    slot = lax.broadcasted_iota(jnp.int32, (LANES // 2, row_count), 0)
    dense = jnp.zeros((LANES // 2, row_count), jnp.float32)
    for k in range(top_count):
        dense += jnp.where(replica_ref[k : k + 1, :] == slot, probability[k : k + 1, :], 0.0)
    high = dense.astype(jnp.bfloat16).astype(jnp.float32)
    low = dense - high
    both = jnp.concatenate([high, low], axis=0)
    both = jnp.concatenate([both, jnp.zeros((LANES, LANES - row_count), jnp.float32)], axis=1)
    out_ref[:, :width] = token_ref[...]
    out_ref[:, width:] = both.T[:row_count].astype(jnp.bfloat16)


def expert_kernel(block_count, *refs):
    slot_ref, gate_ref, up_ref, down_ref = refs[:4]
    blocks = refs[4 : 4 + 2 * block_count]
    away_ref, own_ref, rows_ref, share_ref, hidden_ref = refs[4 + 2 * block_count :]
    row_count = blocks[0].shape[0]
    width, hidden_width = gate_ref.shape[1:]
    half = block_count * row_count
    lane = lax.broadcasted_iota(jnp.int32, (row_count, LANES), 1)
    chosen = (lane == slot_ref[0]) | (lane == slot_ref[0] + LANES // 2)
    for b, block in enumerate(blocks):
        at = pl.ds(b * row_count, row_count)
        rows_ref[at, :] = block[:, :width]
        extra = block[:, width:].astype(jnp.float32)
        share = jnp.sum(jnp.where(chosen, extra, 0.0), axis=1, keepdims=True)
        share_ref[at, :] = jnp.broadcast_to(share, (row_count, LANES))
    rows = rows_ref[...]
    step = 256
    for n in range(0, hidden_width, step):
        gate = jnp.dot(rows, gate_ref[0, :, n : n + step], preferred_element_type=jnp.float32)
        upward = jnp.dot(rows, up_ref[0, :, n : n + step], preferred_element_type=jnp.float32)
        hidden_ref[:, n : n + step] = (gate / (1.0 + jnp.exp(-gate)) * upward).astype(jnp.bfloat16)
    hidden = hidden_ref[...]
    share = share_ref[:, :1]
    for n in range(0, width, step):
        result = jnp.dot(hidden, down_ref[0, :, n : n + step], preferred_element_type=jnp.float32)
        term = result.astype(jnp.bfloat16).astype(jnp.float32) * share
        away_ref[:, n : n + step] = term[:half].astype(jnp.bfloat16)
        own_ref[:, n : n + step] = term[half:]


def pair_kernel(own_ref, other_ref, first_ref, *outs):
    row_count = first_ref.shape[0]
    first_ref[...] = own_ref[:row_count] + other_ref[:row_count].astype(jnp.float32)
    for b, out in enumerate(outs, start=1):
        at = pl.ds(b * row_count, row_count)
        out[...] = (own_ref[at, :] + other_ref[at, :].astype(jnp.float32)).astype(jnp.bfloat16)


def mix_kernel(token_ref, first_ref, *refs):
    total = token_ref[...].astype(jnp.float32) + first_ref[...]
    for ref in refs[:-1]:
        total += ref[...].astype(jnp.float32)
    refs[-1][...] = total.astype(jnp.bfloat16)


def dense_shards(tokens, route_weight, replica, w_gate, w_up, w_down):
    row_count, width = tokens.shape
    hidden_width = w_gate.shape[2]
    peer_count = lax.axis_size("expert")
    pair_count = peer_count // 2
    slot = lax.axis_index("expert").astype(jnp.int32).reshape(1)

    def shift(array, s):
        pairs = [(i, ((i // 2 + s) % pair_count) * 2 + i % 2) for i in range(peer_count)]
        return lax.ppermute(array, "expert", pairs)

    def swap(array):
        return lax.ppermute(array, "expert", [(i, i ^ 1) for i in range(peer_count)])

    packed = pl.pallas_call(
        pack_kernel,
        out_shape=jax.ShapeDtypeStruct((row_count, width + LANES), jnp.bfloat16),
        in_specs=[VMEM] * 3,
        out_specs=VMEM,
        name="pack",
    )(tokens, route_weight.T, replica.T)
    order = list(range(1, pair_count))
    near = [packed] + [shift(packed, s) for s in order]
    far = [swap(block) for block in near]
    total_rows = 2 * pair_count * row_count
    away, own = pl.pallas_call(
        functools.partial(expert_kernel, pair_count),
        out_shape=(
            jax.ShapeDtypeStruct((total_rows // 2, width), jnp.bfloat16),
            jax.ShapeDtypeStruct((total_rows // 2, width), jnp.float32),
        ),
        in_specs=[SMEM] + [VMEM] * (3 + 2 * pair_count),
        out_specs=(VMEM, VMEM),
        scratch_shapes=[
            pltpu.VMEM((total_rows, width), jnp.bfloat16),
            pltpu.VMEM((total_rows, LANES), jnp.float32),
            pltpu.VMEM((total_rows, hidden_width), jnp.bfloat16),
        ],
        compiler_params=pltpu.CompilerParams(vmem_limit_bytes=24 * 2**20),
        name="experts",
    )(slot, in_vmem(w_gate), in_vmem(w_up), in_vmem(w_down), *far, *near)
    other = swap(away)
    block = jax.ShapeDtypeStruct((row_count, width), jnp.bfloat16)
    first, *sums = pl.pallas_call(
        pair_kernel,
        out_shape=(jax.ShapeDtypeStruct((row_count, width), jnp.float32),) + (block,) * (pair_count - 1),
        in_specs=[VMEM] * 2,
        out_specs=(VMEM,) * pair_count,
        compiler_params=pltpu.CompilerParams(vmem_limit_bytes=16 * 2**20),
        name="pair",
    )(own, other)
    back = [shift(array, -s) for s, array in zip(order, sums)]
    return pl.pallas_call(
        mix_kernel,
        out_shape=block,
        in_specs=[VMEM] * (1 + pair_count),
        out_specs=VMEM,
        name="mix",
    )(tokens, first, *back)


def routed_shards(tokens, route_weight, replica, w_gate, w_up, w_down):
    row_count, width = tokens.shape
    top_count = replica.shape[1]
    peer_count = lax.axis_size("expert")
    capacity = min(row_count, max(2, 2 * row_count * top_count // peer_count))
    column_count = w_down.shape[2]
    part_index = lax.axis_index("tensor")
    probability = route_weight / jnp.sum(route_weight, axis=1, keepdims=True)
    flat_slot = replica.reshape(-1)
    one_hot = (flat_slot[:, None] == jnp.arange(peer_count, dtype=jnp.int32)[None, :]).astype(
        jnp.int32
    )
    earlier = jnp.cumsum(one_hot, axis=0) - one_hot
    position = jnp.sum(earlier * one_hot, axis=1)
    source_row = jnp.arange(row_count * top_count, dtype=jnp.int32) // top_count
    own_columns = lax.dynamic_slice_in_dim(tokens, part_index * column_count, column_count, 1)
    outgoing = jnp.zeros((peer_count, capacity, width), jnp.bfloat16)
    outgoing = outgoing.at[flat_slot, position].set(tokens[source_row])
    received = lax.all_to_all(outgoing, "expert", split_axis=0, concat_axis=0, tiled=True)
    slot_rows = received.shape[1]
    flat_rows = received.reshape(-1, width)
    gate = jnp.dot(flat_rows, w_gate[0], preferred_element_type=jnp.float32)
    upward = jnp.dot(flat_rows, w_up[0], preferred_element_type=jnp.float32)
    hidden = (jax.nn.silu(gate) * upward).astype(jnp.bfloat16)
    all_hidden = lax.all_gather(hidden, "tensor", axis=1, tiled=True)
    result = jnp.dot(all_hidden, w_down[0], preferred_element_type=jnp.float32).astype(jnp.bfloat16)
    result = result.reshape(peer_count, slot_rows, column_count)
    returned = lax.all_to_all(result, "expert", split_axis=0, concat_axis=0, tiled=True)
    values = returned[flat_slot, position].astype(jnp.float32)
    weighted = values * probability.reshape(-1)[:, None]
    combined = jnp.sum(weighted.reshape(row_count, top_count, column_count), axis=1)
    return (own_columns.astype(jnp.float32) + combined).astype(jnp.bfloat16)


def shards(*arrays):
    tokens, replica, w_gate = arrays[0], arrays[2], arrays[3]
    row_count, top_count = replica.shape
    peer_count = lax.axis_size("expert")
    if (
        lax.axis_size("tensor") == 1
        and peer_count % 2 == 0
        and 2 <= peer_count <= LANES // 2
        and 2 * top_count >= peer_count
        and row_count % 16 == 0
        and row_count <= LANES
        and tokens.shape[1] % 256 == 0
        and w_gate.shape[2] % 256 == 0
    ):
        return dense_shards(*arrays)
    return routed_shards(*arrays)


def solution(mesh):
    return jax.shard_map(
        shards,
        mesh=mesh,
        in_specs=(
            P(("group", "expert"), None),
            P(("group", "expert"), None),
            P(("group", "expert"), None),
            P("expert", None, "tensor"),
            P("expert", None, "tensor"),
            P("expert", None, "tensor"),
        ),
        out_specs=P(("group", "expert"), "tensor"),
        check_vma=False,
    )
```

```python
import jax
import jax.numpy as jnp
from jax import lax
from jax.experimental import pallas as pl
from jax.experimental.pallas import tpu as pltpu
from jax.sharding import PartitionSpec as P

LANES = 128
VMEM = pl.BlockSpec(memory_space=pltpu.VMEM)
SMEM = pl.BlockSpec(memory_space=pltpu.SMEM)
HBM = pl.BlockSpec(memory_space=pltpu.HBM)


def in_hbm(array):
    return pltpu.with_memory_space_constraint(array, pltpu.HBM)


def pack_kernel(token_ref, weight_hbm, replica_hbm, out_ref, weight_ref, replica_ref, sems):
    width = token_ref.shape[1]
    copies = [
        pltpu.make_async_copy(weight_hbm, weight_ref, sems.at[0]),
        pltpu.make_async_copy(replica_hbm, replica_ref, sems.at[1]),
        pltpu.make_async_copy(token_ref, out_ref.at[:, :width], sems.at[2]),
    ]
    for copy in copies:
        copy.start()
    copies[0].wait()
    copies[1].wait()
    weight = weight_ref[...]
    probability = weight / jnp.sum(weight, axis=0, keepdims=True)
    top_count, row_count = weight.shape
    slot = lax.broadcasted_iota(jnp.int32, (LANES // 2, row_count), 0)
    dense = jnp.zeros((LANES // 2, row_count), jnp.float32)
    for k in range(top_count):
        dense += jnp.where(replica_ref[k : k + 1, :] == slot, probability[k : k + 1, :], 0.0)
    high = dense.astype(jnp.bfloat16).astype(jnp.float32)
    low = dense - high
    both = jnp.concatenate([high, low], axis=0)
    both = jnp.concatenate([both, jnp.zeros((LANES, LANES - row_count), jnp.float32)], axis=1)
    out_ref[:, width:] = both.T[:row_count].astype(jnp.bfloat16)
    copies[2].wait()


def stage_kernel(*refs):
    mark_ref, sems = refs[-2:]
    count = (len(refs) - 3) // 2
    copies = []
    for w, (source, target) in enumerate(zip(refs[1 : 1 + count], refs[1 + count : -2])):
        pieces = sems.shape[1]
        rows = source.shape[1] // pieces
        for p in range(pieces):
            at = pl.ds(p * rows, rows)
            copies.append(pltpu.make_async_copy(source.at[:, at], target.at[:, at], sems.at[w, p]))
    for copy in copies:
        copy.start()
    mark_ref[...] = jnp.zeros_like(mark_ref)
    for copy in copies:
        copy.wait()


def expert_kernel(*refs):
    slot_ref, gate_ref, up_ref, down_ref = refs[:4]
    blocks = refs[4:-5]
    away_ref, own_ref, rows_ref, share_ref, hidden_ref = refs[-5:]
    width, hidden_width = gate_ref.shape[1:]
    half = own_ref.shape[0]
    first = 0
    for block in blocks:
        row_count = block.shape[0]
        at = pl.ds(first, row_count)
        first += row_count
        rows_ref[at, :] = block[:, :width]
        extra = block[:, width:].astype(jnp.float32)
        lane = lax.broadcasted_iota(jnp.int32, extra.shape, 1)
        chosen = (lane == slot_ref[0]) | (lane == slot_ref[0] + LANES // 2)
        share = jnp.sum(jnp.where(chosen, extra, 0.0), axis=1, keepdims=True)
        share_ref[at, :] = jnp.broadcast_to(share, (row_count, LANES))
    rows = rows_ref[...]
    step = 256
    for n in range(0, hidden_width, step):
        gate = jnp.dot(rows, gate_ref[0, :, n : n + step], preferred_element_type=jnp.float32)
        upward = jnp.dot(rows, up_ref[0, :, n : n + step], preferred_element_type=jnp.float32)
        hidden_ref[:, n : n + step] = (gate / (1.0 + jnp.exp(-gate)) * upward).astype(jnp.bfloat16)
    hidden = hidden_ref[...]
    share = share_ref[:, :1]
    for n in range(0, width, step):
        result = jnp.dot(hidden, down_ref[0, :, n : n + step], preferred_element_type=jnp.float32)
        term = result.astype(jnp.bfloat16).astype(jnp.float32) * share
        away_ref[:, n : n + step] = term[:half].astype(jnp.bfloat16)
        own_ref[:, n : n + step] = term[half:]


def join_kernel(*refs):
    row_count = refs[0].shape[0]
    for b, ref in enumerate(refs[:-1]):
        refs[-1][pl.ds(b * row_count, row_count), :] = ref[...]


def pair_kernel(own_ref, other_ref, near_ref, far_ref, *outs):
    row_count = near_ref.shape[0]
    half = own_ref.shape[0] // 2

    def both(b):
        at = pl.ds(b * row_count, row_count)
        return own_ref[at, :] + other_ref[at, :].astype(jnp.float32)

    near_ref[...] = both(0)
    far_ref[...] = both(half // row_count)
    for k, out in enumerate(outs, start=1):
        out[:row_count] = both(k).astype(jnp.bfloat16)
        out[row_count:] = both(half // row_count + k).astype(jnp.bfloat16)


def cross_kernel(far_ref, *refs):
    row_count = far_ref.shape[0]
    total = far_ref[...]
    for ref in refs[:-1]:
        total += ref[row_count:].astype(jnp.float32)
    refs[-1][...] = total.astype(jnp.bfloat16)


def mix_kernel(token_ref, near_ref, crossed_ref, *refs):
    row_count = token_ref.shape[0]
    total = token_ref[...].astype(jnp.float32) + near_ref[...]
    for ref in refs[:-1]:
        total += ref[:row_count].astype(jnp.float32)
    total += crossed_ref[...].astype(jnp.float32)
    refs[-1][...] = total.astype(jnp.bfloat16)


def on_core(kernel, name, outs, ins, scratch=(), limit=8):
    return pl.pallas_call(
        kernel,
        out_shape=outs,
        in_specs=ins,
        out_specs=jax.tree.map(lambda out: VMEM, outs),
        scratch_shapes=list(scratch),
        compiler_params=pltpu.CompilerParams(vmem_limit_bytes=limit * 2**20),
        name=name,
    )


def dense_shards(tokens, route_weight, replica, w_gate, w_up, w_down):
    row_count, width = tokens.shape
    hidden_width = w_gate.shape[2]
    peer_count = lax.axis_size("expert")
    pair_count = peer_count // 2
    half = pair_count // 2
    near_count = half * row_count
    slot = lax.axis_index("expert").astype(jnp.int32).reshape(1)
    wide, full = jnp.bfloat16, jnp.float32

    def partner(array, k):
        return lax.ppermute(array, "expert", [(i, i ^ (2 * k)) for i in range(peer_count)])

    def swap(array):
        return lax.ppermute(array, "expert", [(i, i ^ 1) for i in range(peer_count)])

    def shape(rows, dtype, columns=width):
        return jax.ShapeDtypeStruct((rows, columns), dtype)

    packed = on_core(
        pack_kernel,
        "pack",
        shape(row_count, wide, width + LANES),
        [HBM] * 3,
        (
            pltpu.VMEM(replica.shape[::-1], full),
            pltpu.VMEM(replica.shape[::-1], jnp.int32),
            pltpu.SemaphoreType.DMA((3,)),
        ),
    )(*map(in_hbm, (tokens, route_weight.T, replica.T)))
    crossed = partner(packed, half)
    near = [partner(packed, k) for k in range(1, half)]
    far = [crossed] + [partner(crossed, k) for k in range(1, half)]
    near = [packed] + list(lax.optimization_barrier((crossed, *near)))[1:]
    weights = (w_gate, w_up, w_down)
    *staged, mark = on_core(
        stage_kernel,
        "stage",
        tuple(pltpu.VMEM(w.shape, w.dtype) for w in weights) + (shape(8, full, LANES),),
        [VMEM] + [HBM] * 3,
        (pltpu.SemaphoreType.DMA((3, 4)),),
        limit=2,
    )(crossed, *map(in_hbm, weights))
    far = [crossed] + list(lax.optimization_barrier((mark, *far[1:])))[1:]
    near_rows = shape(near_count, wide, width + LANES)
    other_near = swap(on_core(join_kernel, "join", near_rows, [VMEM] * half)(*near))
    other_far = [swap(block) for block in far]
    total_rows = peer_count * row_count
    inputs = [other_near] + other_far + near + far
    away, own = on_core(
        expert_kernel,
        "experts",
        (shape(total_rows // 2, wide), shape(total_rows // 2, full)),
        [SMEM] + [VMEM] * (3 + len(inputs)),
        (
            pltpu.VMEM((total_rows, width), wide),
            pltpu.VMEM((total_rows, LANES), full),
            pltpu.VMEM((total_rows, hidden_width), wide),
        ),
        limit=24,
    )(slot, *staged, *inputs)
    other = swap(away)
    block, bundle = shape(row_count, full), shape(2 * row_count, wide)
    own_near, own_far, *bundles = on_core(
        pair_kernel, "pair", (block, block) + (bundle,) * (half - 1), [VMEM] * 2, limit=16
    )(own, other)
    arrived = [partner(array, k) for k, array in enumerate(bundles, start=1)]
    send = on_core(cross_kernel, "cross", shape(row_count, wide), [VMEM] * half)(own_far, *arrived)
    crossing = partner(send, half)
    return on_core(mix_kernel, "mix", shape(row_count, wide), [VMEM] * (half + 2))(
        tokens, own_near, crossing, *arrived
    )


def routed_shards(tokens, route_weight, replica, w_gate, w_up, w_down):
    row_count, width = tokens.shape
    top_count = replica.shape[1]
    peer_count = lax.axis_size("expert")
    capacity = min(row_count, max(2, 2 * row_count * top_count // peer_count))
    column_count = w_down.shape[2]
    part_index = lax.axis_index("tensor")
    probability = route_weight / jnp.sum(route_weight, axis=1, keepdims=True)
    flat_slot = replica.reshape(-1)
    one_hot = (flat_slot[:, None] == jnp.arange(peer_count, dtype=jnp.int32)[None, :]).astype(
        jnp.int32
    )
    earlier = jnp.cumsum(one_hot, axis=0) - one_hot
    position = jnp.sum(earlier * one_hot, axis=1)
    source_row = jnp.arange(row_count * top_count, dtype=jnp.int32) // top_count
    own_columns = lax.dynamic_slice_in_dim(tokens, part_index * column_count, column_count, 1)
    outgoing = jnp.zeros((peer_count, capacity, width), jnp.bfloat16)
    outgoing = outgoing.at[flat_slot, position].set(tokens[source_row])
    received = lax.all_to_all(outgoing, "expert", split_axis=0, concat_axis=0, tiled=True)
    slot_rows = received.shape[1]
    flat_rows = received.reshape(-1, width)
    gate = jnp.dot(flat_rows, w_gate[0], preferred_element_type=jnp.float32)
    upward = jnp.dot(flat_rows, w_up[0], preferred_element_type=jnp.float32)
    hidden = (jax.nn.silu(gate) * upward).astype(jnp.bfloat16)
    all_hidden = lax.all_gather(hidden, "tensor", axis=1, tiled=True)
    result = jnp.dot(all_hidden, w_down[0], preferred_element_type=jnp.float32).astype(jnp.bfloat16)
    result = result.reshape(peer_count, slot_rows, column_count)
    returned = lax.all_to_all(result, "expert", split_axis=0, concat_axis=0, tiled=True)
    values = returned[flat_slot, position].astype(jnp.float32)
    weighted = values * probability.reshape(-1)[:, None]
    combined = jnp.sum(weighted.reshape(row_count, top_count, column_count), axis=1)
    return (own_columns.astype(jnp.float32) + combined).astype(jnp.bfloat16)


def shards(*arrays):
    tokens, replica, w_gate = arrays[0], arrays[2], arrays[3]
    row_count, top_count = replica.shape
    peer_count = lax.axis_size("expert")
    if (
        lax.axis_size("tensor") == 1
        and peer_count in (4, 8, 16, 32, 64)
        and 2 * top_count >= peer_count
        and row_count % 16 == 0
        and row_count <= LANES
        and tokens.shape[1] % 256 == 0
        and w_gate.shape[2] % 256 == 0
    ):
        return dense_shards(*arrays)
    return routed_shards(*arrays)


def solution(mesh):
    return jax.shard_map(
        shards,
        mesh=mesh,
        in_specs=(
            P(("group", "expert"), None),
            P(("group", "expert"), None),
            P(("group", "expert"), None),
            P("expert", None, "tensor"),
            P("expert", None, "tensor"),
            P("expert", None, "tensor"),
        ),
        out_specs=P(("group", "expert"), "tensor"),
        check_vma=False,
    )
```

```python
import jax
import jax.numpy as jnp
from jax import lax
from jax.experimental import pallas as pl
from jax.experimental.pallas import tpu as pltpu
from jax.sharding import PartitionSpec as P

LANES = 128
VMEM = pl.BlockSpec(memory_space=pltpu.VMEM)
SMEM = pl.BlockSpec(memory_space=pltpu.SMEM)
HBM = pl.BlockSpec(memory_space=pltpu.HBM)


def in_hbm(array):
    return pltpu.with_memory_space_constraint(array, pltpu.HBM)


def pack_kernel(token_ref, weight_hbm, replica_hbm, out_ref, weight_ref, replica_ref, sems):
    width = token_ref.shape[1]
    copies = [
        pltpu.make_async_copy(weight_hbm, weight_ref, sems.at[0]),
        pltpu.make_async_copy(replica_hbm, replica_ref, sems.at[1]),
        pltpu.make_async_copy(token_ref, out_ref.at[:, :width], sems.at[2]),
    ]
    for copy in copies:
        copy.start()
    copies[0].wait()
    copies[1].wait()
    weight = weight_ref[...]
    probability = weight / jnp.sum(weight, axis=0, keepdims=True)
    top_count, row_count = weight.shape
    slot = lax.broadcasted_iota(jnp.int32, (LANES // 2, row_count), 0)
    dense = jnp.zeros((LANES // 2, row_count), jnp.float32)
    for k in range(top_count):
        dense += jnp.where(replica_ref[k : k + 1, :] == slot, probability[k : k + 1, :], 0.0)
    high = dense.astype(jnp.bfloat16).astype(jnp.float32)
    low = dense - high
    both = jnp.concatenate([high, low], axis=0)
    both = jnp.concatenate([both, jnp.zeros((LANES, LANES - row_count), jnp.float32)], axis=1)
    out_ref[:, width:] = both.T[:row_count].astype(jnp.bfloat16)
    copies[2].wait()


def expert_kernel(*refs):
    slot_ref, gate_ref, up_ref, down_ref = refs[:4]
    blocks = refs[4:-5]
    away_ref, own_ref, rows_ref, share_ref, hidden_ref = refs[-5:]
    width, hidden_width = gate_ref.shape[1:]
    half = own_ref.shape[0]
    first = 0
    for block in blocks:
        row_count = block.shape[0]
        at = pl.ds(first, row_count)
        first += row_count
        rows_ref[at, :] = block[:, :width]
        extra = block[:, width:].astype(jnp.float32)
        lane = lax.broadcasted_iota(jnp.int32, extra.shape, 1)
        chosen = (lane == slot_ref[0]) | (lane == slot_ref[0] + LANES // 2)
        share = jnp.sum(jnp.where(chosen, extra, 0.0), axis=1, keepdims=True)
        share_ref[at, :] = jnp.broadcast_to(share, (row_count, LANES))
    rows = rows_ref[...]
    step = 256
    for n in range(0, hidden_width, step):
        gate = jnp.dot(rows, gate_ref[0, :, n : n + step], preferred_element_type=jnp.float32)
        upward = jnp.dot(rows, up_ref[0, :, n : n + step], preferred_element_type=jnp.float32)
        hidden_ref[:, n : n + step] = (gate / (1.0 + jnp.exp(-gate)) * upward).astype(jnp.bfloat16)
    hidden = hidden_ref[...]
    share = share_ref[:, :1]
    for n in range(0, width, step):
        result = jnp.dot(hidden, down_ref[0, :, n : n + step], preferred_element_type=jnp.float32)
        term = result.astype(jnp.bfloat16).astype(jnp.float32) * share
        away_ref[:, n : n + step] = term[:half].astype(jnp.bfloat16)
        own_ref[:, n : n + step] = term[half:]


def join_kernel(*refs):
    row_count = refs[0].shape[0]
    for b, ref in enumerate(refs[:-1]):
        refs[-1][pl.ds(b * row_count, row_count), :] = ref[...]


def pair_kernel(own_ref, other_ref, first_ref, *outs):
    row_count = first_ref.shape[0]
    for k, out in enumerate((first_ref,) + outs):
        at = pl.ds(k * row_count, row_count)
        total = own_ref[at, :] + other_ref[at, :].astype(jnp.float32)
        out[...] = total.astype(out.dtype)


def sum_kernel(*refs):
    total = refs[0][...].astype(jnp.float32)
    for ref in refs[1:-1]:
        total += ref[...].astype(jnp.float32)
    refs[-1][...] = total.astype(jnp.bfloat16)


def on_core(kernel, name, outs, ins, scratch=(), limit=8, flops=0):
    return pl.pallas_call(
        kernel,
        out_shape=outs,
        in_specs=ins,
        out_specs=jax.tree.map(lambda out: VMEM, outs),
        scratch_shapes=list(scratch),
        compiler_params=pltpu.CompilerParams(vmem_limit_bytes=limit * 2**20),
        cost_estimate=pl.CostEstimate(flops=flops, bytes_accessed=flops // 4096, transcendentals=0),
        name=name,
    )


def dense_shards(tokens, route_weight, replica, w_gate, w_up, w_down):
    row_count, width = tokens.shape
    hidden_width = w_gate.shape[2]
    peer_count = lax.axis_size("expert")
    half = peer_count // 4
    half_rows = half * row_count
    slot = lax.axis_index("expert").astype(jnp.int32).reshape(1)
    wide, full = jnp.bfloat16, jnp.float32

    def partner(array, k):
        return lax.ppermute(array, "expert", [(i, i ^ (2 * k)) for i in range(peer_count)])

    def swap(array):
        return lax.ppermute(array, "expert", [(i, i ^ 1) for i in range(peer_count)])

    def shape(rows, dtype, columns=width):
        return jax.ShapeDtypeStruct((rows, columns), dtype)

    def after(array, *others):
        return lax.optimization_barrier((array, *others))[0]

    def join(blocks):
        rows = shape(half_rows, wide, width + LANES)
        return on_core(join_kernel, "join", rows, [VMEM] * half, flops=10**8)(*blocks)

    def experts(name, blocks):
        return on_core(
            expert_kernel,
            name,
            (shape(half_rows, wide), shape(half_rows, full)),
            [SMEM] + [VMEM] * (3 + len(blocks)),
            (
                pltpu.VMEM((2 * half_rows, width), wide),
                pltpu.VMEM((2 * half_rows, LANES), full),
                pltpu.VMEM((2 * half_rows, hidden_width), wide),
            ),
            limit=16,
            flops=2 * 10**9,
        )(slot, w_gate, w_up, w_down, *blocks)

    def pair(own, other, dtype):
        outs = (shape(row_count, dtype),) + (shape(row_count, wide),) * (half - 1)
        return on_core(pair_kernel, "pair", outs, [VMEM] * 2)(own, other)

    def total(name, *terms):
        return on_core(sum_kernel, name, shape(row_count, wide), [VMEM] * len(terms))(*terms)

    packed = on_core(
        pack_kernel,
        "pack",
        shape(row_count, wide, width + LANES),
        [HBM] * 3,
        (
            pltpu.VMEM(replica.shape[::-1], full),
            pltpu.VMEM(replica.shape[::-1], jnp.int32),
            pltpu.SemaphoreType.DMA((3,)),
        ),
        flops=10**10,
    )(*map(in_hbm, (tokens, route_weight.T, replica.T)))
    crossed = partner(packed, half)
    again = on_core(join_kernel, "again", shape(row_count, wide, width + LANES), [VMEM], flops=10**9)(packed)
    near = [again] + [partner(again, k) for k in range(1, half)]
    far = [crossed] + [partner(crossed, k) for k in range(1, half)]
    near = [after(block, crossed) for block in near]
    near_away, near_own = experts("near", [swap(join(near))] + near)
    far = [crossed] + [after(block, near_away) for block in far[1:]]
    far_away, far_own = experts("far", [swap(block) for block in far] + far)
    far_first, *far_sums = pair(far_own, swap(far_away), full)
    near_first, *near_sums = pair(near_own, swap(near_away), full)
    far_back = [partner(block, k) for k, block in enumerate(far_sums, start=1)]
    near_sums = [after(block, *far_sums) for block in near_sums]
    near_back = [partner(block, k) for k, block in enumerate(near_sums, start=1)]
    crossing = partner(total("cross", far_first, *far_back), half)
    return total("mix", tokens, near_first, *near_back, crossing)


def routed_shards(tokens, route_weight, replica, w_gate, w_up, w_down):
    row_count, width = tokens.shape
    top_count = replica.shape[1]
    peer_count = lax.axis_size("expert")
    capacity = min(row_count, max(2, 2 * row_count * top_count // peer_count))
    column_count = w_down.shape[2]
    part_index = lax.axis_index("tensor")
    probability = route_weight / jnp.sum(route_weight, axis=1, keepdims=True)
    flat_slot = replica.reshape(-1)
    one_hot = (flat_slot[:, None] == jnp.arange(peer_count, dtype=jnp.int32)[None, :]).astype(
        jnp.int32
    )
    earlier = jnp.cumsum(one_hot, axis=0) - one_hot
    position = jnp.sum(earlier * one_hot, axis=1)
    source_row = jnp.arange(row_count * top_count, dtype=jnp.int32) // top_count
    own_columns = lax.dynamic_slice_in_dim(tokens, part_index * column_count, column_count, 1)
    outgoing = jnp.zeros((peer_count, capacity, width), jnp.bfloat16)
    outgoing = outgoing.at[flat_slot, position].set(tokens[source_row])
    received = lax.all_to_all(outgoing, "expert", split_axis=0, concat_axis=0, tiled=True)
    slot_rows = received.shape[1]
    flat_rows = received.reshape(-1, width)
    gate = jnp.dot(flat_rows, w_gate[0], preferred_element_type=jnp.float32)
    upward = jnp.dot(flat_rows, w_up[0], preferred_element_type=jnp.float32)
    hidden = (jax.nn.silu(gate) * upward).astype(jnp.bfloat16)
    all_hidden = lax.all_gather(hidden, "tensor", axis=1, tiled=True)
    result = jnp.dot(all_hidden, w_down[0], preferred_element_type=jnp.float32).astype(jnp.bfloat16)
    result = result.reshape(peer_count, slot_rows, column_count)
    returned = lax.all_to_all(result, "expert", split_axis=0, concat_axis=0, tiled=True)
    values = returned[flat_slot, position].astype(jnp.float32)
    weighted = values * probability.reshape(-1)[:, None]
    combined = jnp.sum(weighted.reshape(row_count, top_count, column_count), axis=1)
    return (own_columns.astype(jnp.float32) + combined).astype(jnp.bfloat16)


def shards(*arrays):
    tokens, replica, w_gate = arrays[0], arrays[2], arrays[3]
    row_count, top_count = replica.shape
    peer_count = lax.axis_size("expert")
    if (
        lax.axis_size("tensor") == 1
        and peer_count in (4, 8, 16, 32, 64)
        and 2 * top_count >= peer_count
        and row_count % 16 == 0
        and row_count <= LANES
        and tokens.shape[1] % 256 == 0
        and w_gate.shape[2] % 256 == 0
    ):
        return dense_shards(*arrays)
    return routed_shards(*arrays)


def solution(mesh):
    return jax.shard_map(
        shards,
        mesh=mesh,
        in_specs=(
            P(("group", "expert"), None),
            P(("group", "expert"), None),
            P(("group", "expert"), None),
            P("expert", None, "tensor"),
            P("expert", None, "tensor"),
            P("expert", None, "tensor"),
        ),
        out_specs=P(("group", "expert"), "tensor"),
        check_vma=False,
    )
```

```python
import jax
import jax.numpy as jnp
from jax import lax
from jax.experimental import pallas as pl
from jax.experimental.pallas import tpu as pltpu
from jax.sharding import PartitionSpec as P

LANES = 128
VMEM = pl.BlockSpec(memory_space=pltpu.VMEM)
HBM = pl.BlockSpec(memory_space=pltpu.HBM)


def in_hbm(array):
    return pltpu.with_memory_space_constraint(array, pltpu.HBM)


def pack_kernel(token_ref, weight_hbm, replica_hbm, out_ref, weight_ref, replica_ref, sems):
    width = token_ref.shape[1]
    copies = [
        pltpu.make_async_copy(weight_hbm, weight_ref, sems.at[0]),
        pltpu.make_async_copy(replica_hbm, replica_ref, sems.at[1]),
        pltpu.make_async_copy(token_ref, out_ref.at[:, :width], sems.at[2]),
    ]
    for copy in copies:
        copy.start()
    copies[0].wait()
    copies[1].wait()
    weight = weight_ref[...]
    probability = weight / jnp.sum(weight, axis=0, keepdims=True)
    top_count, row_count = weight.shape
    slot = lax.broadcasted_iota(jnp.int32, (LANES // 2, row_count), 0)
    dense = jnp.zeros((LANES // 2, row_count), jnp.float32)
    for k in range(top_count):
        dense += jnp.where(replica_ref[k : k + 1, :] == slot, probability[k : k + 1, :], 0.0)
    high = dense.astype(jnp.bfloat16).astype(jnp.float32)
    low = dense - high
    both = jnp.concatenate([high, low], axis=0)
    both = jnp.concatenate([both, jnp.zeros((LANES, LANES - row_count), jnp.float32)], axis=1)
    out_ref[:, width:] = both.T[:row_count].astype(jnp.bfloat16)
    copies[2].wait()


def expert_kernel(*refs):
    gate_ref, up_ref, down_ref = refs[:3]
    blocks = refs[3:-5]
    slot = lax.axis_index("expert")
    away_ref, own_ref, rows_ref, share_ref, hidden_ref = refs[-5:]
    width, hidden_width = gate_ref.shape[1:]
    half = own_ref.shape[0]
    first = 0
    for block in blocks:
        row_count = block.shape[0]
        at = pl.ds(first, row_count)
        first += row_count
        rows_ref[at, :] = block[:, :width]
        extra = block[:, width:].astype(jnp.float32)
        lane = lax.broadcasted_iota(jnp.int32, extra.shape, 1)
        chosen = (lane == slot) | (lane == slot + LANES // 2)
        share = jnp.sum(jnp.where(chosen, extra, 0.0), axis=1, keepdims=True)
        share_ref[at, :] = jnp.broadcast_to(share, (row_count, LANES))
    rows = rows_ref[...]
    step = 256
    for n in range(0, hidden_width, step):
        gate = jnp.dot(rows, gate_ref[0, :, n : n + step], preferred_element_type=jnp.float32)
        upward = jnp.dot(rows, up_ref[0, :, n : n + step], preferred_element_type=jnp.float32)
        hidden_ref[:, n : n + step] = (gate / (1.0 + jnp.exp(-gate)) * upward).astype(jnp.bfloat16)
    hidden = hidden_ref[...]
    share = share_ref[:, :1]
    for n in range(0, width, step):
        result = jnp.dot(hidden, down_ref[0, :, n : n + step], preferred_element_type=jnp.float32)
        term = result.astype(jnp.bfloat16).astype(jnp.float32) * share
        away_ref[:, n : n + step] = term[:half].astype(jnp.bfloat16)
        own_ref[:, n : n + step] = term[half:]


def again_kernel(source_ref, out_ref):
    out_ref[...] = source_ref[...]


def join_kernel(mark_ref, *refs):
    row_count = refs[0].shape[0]
    for b, ref in enumerate(refs[:-1]):
        refs[-1][pl.ds(b * row_count, row_count), :] = ref[...]


def mark_kernel(source_ref, out_ref):
    out_ref[...] = source_ref[:16, :LANES]


def pair_kernel(own_ref, other_ref, first_ref, *outs):
    row_count = first_ref.shape[0]
    for k, out in enumerate((first_ref,) + outs):
        at = pl.ds(k * row_count, row_count)
        total = own_ref[at, :] + other_ref[at, :].astype(jnp.float32)
        out[...] = total.astype(out.dtype)


def sum_kernel(*refs):
    total = refs[0][...].astype(jnp.float32)
    for ref in refs[1:-1]:
        total += ref[...].astype(jnp.float32)
    refs[-1][...] = total.astype(jnp.bfloat16)


def on_core(kernel, name, outs, ins, scratch=(), limit=8, flops=0):
    return pl.pallas_call(
        kernel,
        out_shape=outs,
        in_specs=ins,
        out_specs=jax.tree.map(lambda out: VMEM, outs),
        scratch_shapes=list(scratch),
        compiler_params=pltpu.CompilerParams(vmem_limit_bytes=limit * 2**20),
        cost_estimate=pl.CostEstimate(flops=flops, bytes_accessed=flops // 4096, transcendentals=0),
        name=name,
    )


def dense_shards(tokens, route_weight, replica, w_gate, w_up, w_down):
    row_count, width = tokens.shape
    hidden_width = w_gate.shape[2]
    peer_count = lax.axis_size("expert")
    half = peer_count // 4
    half_rows = half * row_count
    wide, full = jnp.bfloat16, jnp.float32

    def partner(array, k):
        return lax.ppermute(array, "expert", [(i, i ^ (2 * k)) for i in range(peer_count)])

    def swap(array):
        return lax.ppermute(array, "expert", [(i, i ^ 1) for i in range(peer_count)])

    def shape(rows, dtype, columns=width):
        return jax.ShapeDtypeStruct((rows, columns), dtype)

    def after(array, *others):
        return lax.optimization_barrier((array, *others))[0]

    def join(blocks, mark):
        rows = shape(half_rows, wide, width + LANES)
        return on_core(join_kernel, "join", rows, [VMEM] * (half + 1), flops=10**8)(mark, *blocks)

    def experts(name, blocks):
        return on_core(
            expert_kernel,
            name,
            (shape(half_rows, wide), shape(half_rows, full)),
            [VMEM] * (3 + len(blocks)),
            (
                pltpu.VMEM((2 * half_rows, width), wide),
                pltpu.VMEM((2 * half_rows, LANES), full),
                pltpu.VMEM((2 * half_rows, hidden_width), wide),
            ),
            limit=16,
            flops=10**9,
        )(w_gate, w_up, w_down, *blocks)

    def pair(own, other, dtype):
        outs = (shape(row_count, dtype),) + (shape(row_count, wide),) * (half - 1)
        return on_core(pair_kernel, "pair", outs, [VMEM] * 2)(own, other)

    def total(name, *terms):
        return on_core(sum_kernel, name, shape(row_count, wide), [VMEM] * len(terms))(*terms)

    packed = on_core(
        pack_kernel,
        "pack",
        shape(row_count, wide, width + LANES),
        [HBM] * 3,
        (
            pltpu.VMEM(replica.shape[::-1], full),
            pltpu.VMEM(replica.shape[::-1], jnp.int32),
            pltpu.SemaphoreType.DMA((3,)),
        ),
        flops=10**10,
    )(*map(in_hbm, (tokens, route_weight.T, replica.T)))
    crossed = partner(packed, half)
    again = on_core(again_kernel, "again", shape(row_count, wide, width + LANES), [VMEM], flops=10**9)(packed)
    near = [again] + [partner(again, k) for k in range(1, half)]
    far = [crossed] + [partner(crossed, k) for k in range(1, half)]
    crossed_other = swap(crossed)
    mark = on_core(mark_kernel, "mark", shape(16, wide, LANES), [VMEM], flops=10**9)(crossed)
    near_away, near_own = experts("near", [swap(join(near, mark))] + near)
    far = [crossed] + [after(block, near_away) for block in far[1:]]
    far_other = [crossed_other] + [swap(block) for block in far[1:]]
    far_away, far_own = experts("far", far_other + far)
    far_first, *far_sums = pair(far_own, swap(far_away), full)
    near_first, *near_sums = pair(near_own, swap(near_away), full)
    far_back = [partner(block, k) for k, block in enumerate(far_sums, start=1)]
    near_sums = [after(block, *far_sums) for block in near_sums]
    near_back = [partner(block, k) for k, block in enumerate(near_sums, start=1)]
    crossing = partner(total("cross", far_first, *far_back), half)
    return total("mix", tokens, near_first, *near_back, crossing)


def routed_shards(tokens, route_weight, replica, w_gate, w_up, w_down):
    row_count, width = tokens.shape
    top_count = replica.shape[1]
    peer_count = lax.axis_size("expert")
    capacity = min(row_count, max(2, 2 * row_count * top_count // peer_count))
    column_count = w_down.shape[2]
    part_index = lax.axis_index("tensor")
    probability = route_weight / jnp.sum(route_weight, axis=1, keepdims=True)
    flat_slot = replica.reshape(-1)
    one_hot = (flat_slot[:, None] == jnp.arange(peer_count, dtype=jnp.int32)[None, :]).astype(
        jnp.int32
    )
    earlier = jnp.cumsum(one_hot, axis=0) - one_hot
    position = jnp.sum(earlier * one_hot, axis=1)
    source_row = jnp.arange(row_count * top_count, dtype=jnp.int32) // top_count
    own_columns = lax.dynamic_slice_in_dim(tokens, part_index * column_count, column_count, 1)
    outgoing = jnp.zeros((peer_count, capacity, width), jnp.bfloat16)
    outgoing = outgoing.at[flat_slot, position].set(tokens[source_row])
    received = lax.all_to_all(outgoing, "expert", split_axis=0, concat_axis=0, tiled=True)
    slot_rows = received.shape[1]
    flat_rows = received.reshape(-1, width)
    gate = jnp.dot(flat_rows, w_gate[0], preferred_element_type=jnp.float32)
    upward = jnp.dot(flat_rows, w_up[0], preferred_element_type=jnp.float32)
    hidden = (jax.nn.silu(gate) * upward).astype(jnp.bfloat16)
    all_hidden = lax.all_gather(hidden, "tensor", axis=1, tiled=True)
    result = jnp.dot(all_hidden, w_down[0], preferred_element_type=jnp.float32).astype(jnp.bfloat16)
    result = result.reshape(peer_count, slot_rows, column_count)
    returned = lax.all_to_all(result, "expert", split_axis=0, concat_axis=0, tiled=True)
    values = returned[flat_slot, position].astype(jnp.float32)
    weighted = values * probability.reshape(-1)[:, None]
    combined = jnp.sum(weighted.reshape(row_count, top_count, column_count), axis=1)
    return (own_columns.astype(jnp.float32) + combined).astype(jnp.bfloat16)


def shards(*arrays):
    tokens, replica, w_gate = arrays[0], arrays[2], arrays[3]
    row_count, top_count = replica.shape
    peer_count = lax.axis_size("expert")
    if (
        lax.axis_size("tensor") == 1
        and peer_count in (4, 8, 16, 32, 64)
        and 2 * top_count >= peer_count
        and row_count % 16 == 0
        and row_count <= LANES
        and tokens.shape[1] % 256 == 0
        and w_gate.shape[2] % 256 == 0
    ):
        return dense_shards(*arrays)
    return routed_shards(*arrays)


def solution(mesh):
    return jax.shard_map(
        shards,
        mesh=mesh,
        in_specs=(
            P(("group", "expert"), None),
            P(("group", "expert"), None),
            P(("group", "expert"), None),
            P("expert", None, "tensor"),
            P("expert", None, "tensor"),
            P("expert", None, "tensor"),
        ),
        out_specs=P(("group", "expert"), "tensor"),
        check_vma=False,
    )
```

```python
import functools
import jax
import jax.numpy as jnp
from jax import lax
from jax.experimental import pallas as pl
from jax.experimental.pallas import tpu as pltpu
from jax.sharding import PartitionSpec as P

LANES = 128
VMEM = pl.BlockSpec(memory_space=pltpu.VMEM)
HBM = pl.BlockSpec(memory_space=pltpu.HBM)


def in_hbm(array):
    return pltpu.with_memory_space_constraint(array, pltpu.HBM)


def pack_kernel(token_ref, weight_hbm, replica_hbm, out_ref, weight_ref, replica_ref, sems):
    width = token_ref.shape[1]
    copies = [
        pltpu.make_async_copy(weight_hbm, weight_ref, sems.at[0]),
        pltpu.make_async_copy(replica_hbm, replica_ref, sems.at[1]),
        pltpu.make_async_copy(token_ref, out_ref.at[:, :width], sems.at[2]),
    ]
    for copy in copies:
        copy.start()
    copies[0].wait()
    copies[1].wait()
    weight = weight_ref[...]
    probability = weight / jnp.sum(weight, axis=0, keepdims=True)
    top_count, row_count = weight.shape
    slot = lax.broadcasted_iota(jnp.int32, (LANES // 2, row_count), 0)
    dense = jnp.zeros((LANES // 2, row_count), jnp.float32)
    for k in range(top_count):
        dense += jnp.where(replica_ref[k : k + 1, :] == slot, probability[k : k + 1, :], 0.0)
    high = dense.astype(jnp.bfloat16).astype(jnp.float32)
    low = dense - high
    both = jnp.concatenate([high, low], axis=0)
    both = jnp.concatenate([both, jnp.zeros((LANES, LANES - row_count), jnp.float32)], axis=1)
    out_ref[:, width:] = both.T[:row_count].astype(jnp.bfloat16)
    copies[2].wait()


def expert_kernel(block_count, *refs):
    gate_ref, up_ref, down_ref = refs[:3]
    blocks = refs[3 : 3 + block_count]
    slot = lax.axis_index("expert")
    away_ref, own_ref, rows_ref, share_ref, hidden_ref = refs[-5:]
    width, hidden_width = gate_ref.shape[1:]
    half = own_ref.shape[0]
    first = 0
    for block in blocks:
        row_count = block.shape[0]
        at = pl.ds(first, row_count)
        first += row_count
        rows_ref[at, :] = block[:, :width]
        extra = block[:, width:].astype(jnp.float32)
        lane = lax.broadcasted_iota(jnp.int32, extra.shape, 1)
        chosen = (lane == slot) | (lane == slot + LANES // 2)
        share = jnp.sum(jnp.where(chosen, extra, 0.0), axis=1, keepdims=True)
        share_ref[at, :] = jnp.broadcast_to(share, (row_count, LANES))
    rows = rows_ref[...]
    step = 256
    for n in range(0, hidden_width, step):
        gate = jnp.dot(rows, gate_ref[0, :, n : n + step], preferred_element_type=jnp.float32)
        upward = jnp.dot(rows, up_ref[0, :, n : n + step], preferred_element_type=jnp.float32)
        hidden_ref[:, n : n + step] = (gate / (1.0 + jnp.exp(-gate)) * upward).astype(jnp.bfloat16)
    hidden = hidden_ref[...]
    share = share_ref[:, :1]
    for n in range(0, width, step):
        result = jnp.dot(hidden, down_ref[0, :, n : n + step], preferred_element_type=jnp.float32)
        term = result.astype(jnp.bfloat16).astype(jnp.float32) * share
        away_ref[:, n : n + step] = term[:half].astype(jnp.bfloat16)
        own_ref[:, n : n + step] = term[half:]


def again_kernel(source_ref, out_ref):
    out_ref[...] = source_ref[...]


def join_kernel(*refs):
    row_count = refs[0].shape[0]
    for b, ref in enumerate(refs[: refs[-1].shape[0] // row_count]):
        refs[-1][pl.ds(b * row_count, row_count), :] = ref[...]


def pair_kernel(own_ref, other_ref, first_ref, *outs):
    row_count = first_ref.shape[0]
    for k, out in enumerate((first_ref,) + outs):
        at = pl.ds(k * row_count, row_count)
        total = own_ref[at, :] + other_ref[at, :].astype(jnp.float32)
        out[...] = total.astype(out.dtype)


def sum_kernel(*refs):
    total = refs[0][...].astype(jnp.float32)
    for ref in refs[1:-1]:
        total += ref[...].astype(jnp.float32)
    refs[-1][...] = total.astype(jnp.bfloat16)


def on_core(kernel, name, outs, ins, scratch=(), limit=8, flops=0):
    return pl.pallas_call(
        kernel,
        out_shape=outs,
        in_specs=ins,
        out_specs=jax.tree.map(lambda out: VMEM, outs),
        scratch_shapes=list(scratch),
        compiler_params=pltpu.CompilerParams(vmem_limit_bytes=limit * 2**20),
        cost_estimate=pl.CostEstimate(flops=flops, bytes_accessed=flops // 4096, transcendentals=0),
        name=name,
    )


def dense_shards(tokens, route_weight, replica, w_gate, w_up, w_down):
    row_count, width = tokens.shape
    hidden_width = w_gate.shape[2]
    peer_count = lax.axis_size("expert")
    half = peer_count // 4
    half_rows = half * row_count
    wide, full = jnp.bfloat16, jnp.float32

    def partner(array, k):
        return lax.ppermute(array, "expert", [(i, i ^ (2 * k)) for i in range(peer_count)])

    def swap(array):
        return lax.ppermute(array, "expert", [(i, i ^ 1) for i in range(peer_count)])

    def shape(rows, dtype, columns=width):
        return jax.ShapeDtypeStruct((rows, columns), dtype)

    def after(array, *others):
        return lax.optimization_barrier((array, *others))[0]

    def join(blocks, marks):
        rows = shape(half_rows, wide, width + LANES)
        refs = (*blocks, *marks)
        return on_core(join_kernel, "join", rows, [VMEM] * len(refs), flops=10**8)(*refs)

    def experts(name, blocks, marks=()):
        return on_core(
            functools.partial(expert_kernel, len(blocks)),
            name,
            (shape(half_rows, wide), shape(half_rows, full)),
            [VMEM] * (3 + len(blocks) + len(marks)),
            (
                pltpu.VMEM((2 * half_rows, width), wide),
                pltpu.VMEM((2 * half_rows, LANES), full),
                pltpu.VMEM((2 * half_rows, hidden_width), wide),
            ),
            limit=16,
            flops=10**9,
        )(w_gate, w_up, w_down, *blocks, *marks)

    def pair(own, other, dtype):
        outs = (shape(row_count, dtype),) + (shape(row_count, wide),) * (half - 1)
        return on_core(pair_kernel, "pair", outs, [VMEM] * 2)(own, other)

    def total(name, *terms):
        return on_core(sum_kernel, name, shape(row_count, wide), [VMEM] * len(terms))(*terms)

    packed = on_core(
        pack_kernel,
        "pack",
        shape(row_count, wide, width + LANES),
        [HBM] * 3,
        (
            pltpu.VMEM(replica.shape[::-1], full),
            pltpu.VMEM(replica.shape[::-1], jnp.int32),
            pltpu.SemaphoreType.DMA((3,)),
        ),
        flops=10**10,
    )(*map(in_hbm, (tokens, route_weight.T, replica.T)))
    crossed = partner(packed, half)
    again = on_core(again_kernel, "again", shape(row_count, wide, width + LANES), [VMEM], flops=10**9)(packed)
    near = [again] + [partner(again, k) for k in range(1, half)]
    far = [crossed] + [partner(crossed, k) for k in range(1, half)]
    crossed_other = swap(crossed)
    near_other = [swap(block) for block in near]
    near_away, near_own = experts("near", near_other + near, far[1:4])
    far_other = [crossed_other] + [swap(block) for block in far[1:]]
    far_away, far_own = experts("far", far_other + far)
    far_first, *far_sums = pair(far_own, swap(far_away), full)
    near_first, *near_sums = pair(near_own, swap(near_away), full)
    far_back = [partner(block, k) for k, block in enumerate(far_sums, start=1)]
    near_sums = [after(block, *far_sums) for block in near_sums]
    near_back = [partner(block, k) for k, block in enumerate(near_sums, start=1)]
    crossing = partner(total("cross", far_first, *far_back), half)
    return total("mix", tokens, near_first, *near_back, crossing)


def routed_shards(tokens, route_weight, replica, w_gate, w_up, w_down):
    row_count, width = tokens.shape
    top_count = replica.shape[1]
    peer_count = lax.axis_size("expert")
    capacity = min(row_count, max(2, 2 * row_count * top_count // peer_count))
    column_count = w_down.shape[2]
    part_index = lax.axis_index("tensor")
    probability = route_weight / jnp.sum(route_weight, axis=1, keepdims=True)
    flat_slot = replica.reshape(-1)
    one_hot = (flat_slot[:, None] == jnp.arange(peer_count, dtype=jnp.int32)[None, :]).astype(
        jnp.int32
    )
    earlier = jnp.cumsum(one_hot, axis=0) - one_hot
    position = jnp.sum(earlier * one_hot, axis=1)
    source_row = jnp.arange(row_count * top_count, dtype=jnp.int32) // top_count
    own_columns = lax.dynamic_slice_in_dim(tokens, part_index * column_count, column_count, 1)
    outgoing = jnp.zeros((peer_count, capacity, width), jnp.bfloat16)
    outgoing = outgoing.at[flat_slot, position].set(tokens[source_row])
    received = lax.all_to_all(outgoing, "expert", split_axis=0, concat_axis=0, tiled=True)
    slot_rows = received.shape[1]
    flat_rows = received.reshape(-1, width)
    gate = jnp.dot(flat_rows, w_gate[0], preferred_element_type=jnp.float32)
    upward = jnp.dot(flat_rows, w_up[0], preferred_element_type=jnp.float32)
    hidden = (jax.nn.silu(gate) * upward).astype(jnp.bfloat16)
    all_hidden = lax.all_gather(hidden, "tensor", axis=1, tiled=True)
    result = jnp.dot(all_hidden, w_down[0], preferred_element_type=jnp.float32).astype(jnp.bfloat16)
    result = result.reshape(peer_count, slot_rows, column_count)
    returned = lax.all_to_all(result, "expert", split_axis=0, concat_axis=0, tiled=True)
    values = returned[flat_slot, position].astype(jnp.float32)
    weighted = values * probability.reshape(-1)[:, None]
    combined = jnp.sum(weighted.reshape(row_count, top_count, column_count), axis=1)
    return (own_columns.astype(jnp.float32) + combined).astype(jnp.bfloat16)


def shards(*arrays):
    tokens, replica, w_gate = arrays[0], arrays[2], arrays[3]
    row_count, top_count = replica.shape
    peer_count = lax.axis_size("expert")
    if (
        lax.axis_size("tensor") == 1
        and peer_count in (4, 8, 16, 32, 64)
        and 2 * top_count >= peer_count
        and row_count % 16 == 0
        and row_count <= LANES
        and tokens.shape[1] % 256 == 0
        and w_gate.shape[2] % 256 == 0
    ):
        return dense_shards(*arrays)
    return routed_shards(*arrays)


def solution(mesh):
    return jax.shard_map(
        shards,
        mesh=mesh,
        in_specs=(
            P(("group", "expert"), None),
            P(("group", "expert"), None),
            P(("group", "expert"), None),
            P("expert", None, "tensor"),
            P("expert", None, "tensor"),
            P("expert", None, "tensor"),
        ),
        out_specs=P(("group", "expert"), "tensor"),
        check_vma=False,
    )
```

```python
import functools
import jax
import jax.numpy as jnp
from jax import lax
from jax.experimental import pallas as pl
from jax.experimental.pallas import tpu as pltpu
from jax.sharding import PartitionSpec as P

LANES = 128
VMEM = pl.BlockSpec(memory_space=pltpu.VMEM)
HBM = pl.BlockSpec(memory_space=pltpu.HBM)


def in_hbm(array):
    return pltpu.with_memory_space_constraint(array, pltpu.HBM)


def pack_kernel(token_ref, weight_hbm, replica_hbm, out_ref, weight_ref, replica_ref, sems):
    width = token_ref.shape[1]
    copies = [
        pltpu.make_async_copy(weight_hbm, weight_ref, sems.at[0]),
        pltpu.make_async_copy(replica_hbm, replica_ref, sems.at[1]),
        pltpu.make_async_copy(token_ref, out_ref.at[:, :width], sems.at[2]),
    ]
    for copy in copies:
        copy.start()
    copies[0].wait()
    copies[1].wait()
    weight = weight_ref[...]
    probability = weight / jnp.sum(weight, axis=0, keepdims=True)
    top_count, row_count = weight.shape
    slot = lax.broadcasted_iota(jnp.int32, (LANES // 2, row_count), 0)
    dense = jnp.zeros((LANES // 2, row_count), jnp.float32)
    for k in range(top_count):
        dense += jnp.where(replica_ref[k : k + 1, :] == slot, probability[k : k + 1, :], 0.0)
    high = dense.astype(jnp.bfloat16).astype(jnp.float32)
    low = dense - high
    both = jnp.concatenate([high, low], axis=0)
    both = jnp.concatenate([both, jnp.zeros((LANES, LANES - row_count), jnp.float32)], axis=1)
    out_ref[:, width:] = both.T[:row_count].astype(jnp.bfloat16)
    copies[2].wait()


def expert_kernel(block_count, *refs):
    gate_ref, up_ref, down_ref = refs[:3]
    blocks = refs[3 : 3 + block_count]
    slot = lax.axis_index("expert")
    away_ref, own_ref, rows_ref, share_ref, hidden_ref = refs[-5:]
    width, hidden_width = gate_ref.shape[1:]
    half = own_ref.shape[0]
    first = 0
    for block in blocks:
        row_count = block.shape[0]
        at = pl.ds(first, row_count)
        first += row_count
        rows_ref[at, :] = block[:, :width]
        extra = block[:, width:].astype(jnp.float32)
        lane = lax.broadcasted_iota(jnp.int32, extra.shape, 1)
        chosen = (lane == slot) | (lane == slot + LANES // 2)
        share = jnp.sum(jnp.where(chosen, extra, 0.0), axis=1, keepdims=True)
        share_ref[at, :] = jnp.broadcast_to(share, (row_count, LANES))
    rows = rows_ref[...]
    step = 256
    for n in range(0, hidden_width, step):
        gate = jnp.dot(rows, gate_ref[0, :, n : n + step], preferred_element_type=jnp.float32)
        upward = jnp.dot(rows, up_ref[0, :, n : n + step], preferred_element_type=jnp.float32)
        hidden_ref[:, n : n + step] = (gate / (1.0 + jnp.exp(-gate)) * upward).astype(jnp.bfloat16)
    hidden = hidden_ref[...]
    share = share_ref[:, :1]
    for n in range(0, width, step):
        result = jnp.dot(hidden, down_ref[0, :, n : n + step], preferred_element_type=jnp.float32)
        term = result.astype(jnp.bfloat16).astype(jnp.float32) * share
        away_ref[:, n : n + step] = term[:half].astype(jnp.bfloat16)
        own_ref[:, n : n + step] = term[half:]


def again_kernel(source_ref, out_ref):
    out_ref[...] = source_ref[...]


def pair_kernel(own_ref, other_ref, first_ref, *outs):
    row_count = first_ref.shape[0]
    for k, out in enumerate((first_ref,) + outs):
        at = pl.ds(k * row_count, row_count)
        total = own_ref[at, :] + other_ref[at, :].astype(jnp.float32)
        out[...] = total.astype(out.dtype)


def sum_kernel(*refs):
    total = refs[0][...].astype(jnp.float32)
    for ref in refs[1:-1]:
        total += ref[...].astype(jnp.float32)
    refs[-1][...] = total.astype(jnp.bfloat16)


def on_core(kernel, name, outs, ins, scratch=(), limit=8, flops=0):
    return pl.pallas_call(
        kernel,
        out_shape=outs,
        in_specs=ins,
        out_specs=jax.tree.map(lambda out: VMEM, outs),
        scratch_shapes=list(scratch),
        compiler_params=pltpu.CompilerParams(vmem_limit_bytes=limit * 2**20),
        cost_estimate=pl.CostEstimate(flops=flops, bytes_accessed=flops // 4096, transcendentals=0),
        name=name,
    )


def dense_shards(tokens, route_weight, replica, w_gate, w_up, w_down):
    row_count, width = tokens.shape
    hidden_width = w_gate.shape[2]
    peer_count = lax.axis_size("expert")
    half = peer_count // 4
    half_rows = half * row_count
    wide, full = jnp.bfloat16, jnp.float32

    def partner(array, k):
        return lax.ppermute(array, "expert", [(i, i ^ (2 * k)) for i in range(peer_count)])

    def swap(array):
        return lax.ppermute(array, "expert", [(i, i ^ 1) for i in range(peer_count)])

    def shape(rows, dtype, columns=width):
        return jax.ShapeDtypeStruct((rows, columns), dtype)

    def experts(name, blocks, marks=()):
        return on_core(
            functools.partial(expert_kernel, len(blocks)),
            name,
            (shape(half_rows, wide), shape(half_rows, full)),
            [VMEM] * (3 + len(blocks) + len(marks)),
            (
                pltpu.VMEM((2 * half_rows, width), wide),
                pltpu.VMEM((2 * half_rows, LANES), full),
                pltpu.VMEM((2 * half_rows, hidden_width), wide),
            ),
            limit=16,
            flops=10**9,
        )(w_gate, w_up, w_down, *blocks, *marks)

    def pair(own, other, dtype):
        outs = (shape(row_count, dtype),) + (shape(row_count, wide),) * (half - 1)
        return on_core(pair_kernel, "pair", outs, [VMEM] * 2)(own, other)

    def total(name, *terms):
        return on_core(sum_kernel, name, shape(row_count, wide), [VMEM] * len(terms))(*terms)

    packed = on_core(
        pack_kernel,
        "pack",
        shape(row_count, wide, width + LANES),
        [HBM] * 3,
        (
            pltpu.VMEM(replica.shape[::-1], full),
            pltpu.VMEM(replica.shape[::-1], jnp.int32),
            pltpu.SemaphoreType.DMA((3,)),
        ),
        flops=10**10,
    )(*map(in_hbm, (tokens, route_weight.T, replica.T)))
    crossed = partner(packed, half)
    again = on_core(again_kernel, "again", shape(row_count, wide, width + LANES), [VMEM], flops=10**9)(packed)
    order = range(half - 1, 0, -1)
    near = [again] + [partner(again, k) for k in order]
    far = [crossed] + [partner(crossed, k) for k in order]
    crossed_other = swap(crossed)
    near_other = [swap(block) for block in near]
    near_away, near_own = experts("near", near_other + near, far[1:])
    far_other = [crossed_other] + [swap(block) for block in far[1:]]
    far_away, far_own = experts("far", far_other + far)
    far_first, *far_sums = pair(far_own, swap(far_away), full)
    near_first, *near_sums = pair(near_own, swap(near_away), full)
    far_back = [partner(block, k) for block, k in zip(far_sums, order)]
    near_back = [partner(block, k) for block, k in zip(near_sums, order)]
    crossing = partner(total("cross", far_first, *far_back), half)
    return total("mix", tokens, near_first, *near_back, crossing)


def routed_shards(tokens, route_weight, replica, w_gate, w_up, w_down):
    row_count, width = tokens.shape
    top_count = replica.shape[1]
    peer_count = lax.axis_size("expert")
    capacity = min(row_count, max(2, 2 * row_count * top_count // peer_count))
    column_count = w_down.shape[2]
    part_index = lax.axis_index("tensor")
    probability = route_weight / jnp.sum(route_weight, axis=1, keepdims=True)
    flat_slot = replica.reshape(-1)
    one_hot = (flat_slot[:, None] == jnp.arange(peer_count, dtype=jnp.int32)[None, :]).astype(
        jnp.int32
    )
    earlier = jnp.cumsum(one_hot, axis=0) - one_hot
    position = jnp.sum(earlier * one_hot, axis=1)
    source_row = jnp.arange(row_count * top_count, dtype=jnp.int32) // top_count
    own_columns = lax.dynamic_slice_in_dim(tokens, part_index * column_count, column_count, 1)
    outgoing = jnp.zeros((peer_count, capacity, width), jnp.bfloat16)
    outgoing = outgoing.at[flat_slot, position].set(tokens[source_row])
    received = lax.all_to_all(outgoing, "expert", split_axis=0, concat_axis=0, tiled=True)
    slot_rows = received.shape[1]
    flat_rows = received.reshape(-1, width)
    gate = jnp.dot(flat_rows, w_gate[0], preferred_element_type=jnp.float32)
    upward = jnp.dot(flat_rows, w_up[0], preferred_element_type=jnp.float32)
    hidden = (jax.nn.silu(gate) * upward).astype(jnp.bfloat16)
    all_hidden = lax.all_gather(hidden, "tensor", axis=1, tiled=True)
    result = jnp.dot(all_hidden, w_down[0], preferred_element_type=jnp.float32).astype(jnp.bfloat16)
    result = result.reshape(peer_count, slot_rows, column_count)
    returned = lax.all_to_all(result, "expert", split_axis=0, concat_axis=0, tiled=True)
    values = returned[flat_slot, position].astype(jnp.float32)
    weighted = values * probability.reshape(-1)[:, None]
    combined = jnp.sum(weighted.reshape(row_count, top_count, column_count), axis=1)
    return (own_columns.astype(jnp.float32) + combined).astype(jnp.bfloat16)


def shards(*arrays):
    tokens, replica, w_gate = arrays[0], arrays[2], arrays[3]
    row_count, top_count = replica.shape
    peer_count = lax.axis_size("expert")
    if (
        lax.axis_size("tensor") == 1
        and peer_count in (4, 8, 16, 32, 64)
        and 2 * top_count >= peer_count
        and row_count % 16 == 0
        and row_count <= LANES
        and tokens.shape[1] % 256 == 0
        and w_gate.shape[2] % 256 == 0
    ):
        return dense_shards(*arrays)
    return routed_shards(*arrays)


def solution(mesh):
    return jax.shard_map(
        shards,
        mesh=mesh,
        in_specs=(
            P(("group", "expert"), None),
            P(("group", "expert"), None),
            P(("group", "expert"), None),
            P("expert", None, "tensor"),
            P("expert", None, "tensor"),
            P("expert", None, "tensor"),
        ),
        out_specs=P(("group", "expert"), "tensor"),
        check_vma=False,
    )
```

```python
import functools
import jax
import jax.numpy as jnp
from jax import lax
from jax.experimental import pallas as pl
from jax.experimental.pallas import tpu as pltpu
from jax.sharding import PartitionSpec as P

LANES = 128
VMEM = pl.BlockSpec(memory_space=pltpu.VMEM)
HBM = pl.BlockSpec(memory_space=pltpu.HBM)


def in_hbm(array):
    return pltpu.with_memory_space_constraint(array, pltpu.HBM)


def pack_kernel(token_ref, weight_hbm, replica_hbm, out_ref, weight_ref, replica_ref, sems):
    width = token_ref.shape[1]
    copies = [
        pltpu.make_async_copy(weight_hbm, weight_ref, sems.at[0]),
        pltpu.make_async_copy(replica_hbm, replica_ref, sems.at[1]),
        pltpu.make_async_copy(token_ref, out_ref.at[:, :width], sems.at[2]),
    ]
    for copy in copies:
        copy.start()
    copies[0].wait()
    copies[1].wait()
    weight = weight_ref[...]
    probability = weight / jnp.sum(weight, axis=0, keepdims=True)
    top_count, row_count = weight.shape
    slot = lax.broadcasted_iota(jnp.int32, (LANES // 2, row_count), 0)
    dense = jnp.zeros((LANES // 2, row_count), jnp.float32)
    for k in range(top_count):
        dense += jnp.where(replica_ref[k : k + 1, :] == slot, probability[k : k + 1, :], 0.0)
    high = dense.astype(jnp.bfloat16).astype(jnp.float32)
    low = dense - high
    both = jnp.concatenate([high, low], axis=0)
    both = jnp.concatenate([both, jnp.zeros((LANES, LANES - row_count), jnp.float32)], axis=1)
    out_ref[:, width:] = both.T[:row_count].astype(jnp.bfloat16)
    copies[2].wait()


def expert_kernel(block_count, *refs):
    gate_ref, up_ref, down_ref = refs[:3]
    blocks = refs[3 : 3 + block_count]
    slot = lax.axis_index("expert")
    away_ref, own_ref, rows_ref, share_ref, hidden_ref = refs[-5:]
    width, hidden_width = gate_ref.shape[1:]
    half = own_ref.shape[0]
    first = 0
    for block in blocks:
        row_count = block.shape[0]
        at = pl.ds(first, row_count)
        first += row_count
        rows_ref[at, :] = block[:, :width]
        extra = block[:, width:].astype(jnp.float32)
        lane = lax.broadcasted_iota(jnp.int32, extra.shape, 1)
        chosen = (lane == slot) | (lane == slot + LANES // 2)
        share = jnp.sum(jnp.where(chosen, extra, 0.0), axis=1, keepdims=True)
        share_ref[at, :] = jnp.broadcast_to(share, (row_count, LANES))
    rows = rows_ref[...]
    step = 256
    for n in range(0, hidden_width, step):
        gate = jnp.dot(rows, gate_ref[0, :, n : n + step], preferred_element_type=jnp.float32)
        upward = jnp.dot(rows, up_ref[0, :, n : n + step], preferred_element_type=jnp.float32)
        hidden_ref[:, n : n + step] = (gate / (1.0 + jnp.exp(-gate)) * upward).astype(jnp.bfloat16)
    hidden = hidden_ref[...]
    share = share_ref[:, :1]
    for n in range(0, width, step):
        result = jnp.dot(hidden, down_ref[0, :, n : n + step], preferred_element_type=jnp.float32)
        term = result.astype(jnp.bfloat16).astype(jnp.float32) * share
        away_ref[:, n : n + step] = term[:half].astype(jnp.bfloat16)
        own_ref[:, n : n + step] = term[half:]


def again_kernel(source_ref, out_ref):
    out_ref[...] = source_ref[...]


def join_kernel(*refs):
    row_count = refs[0].shape[0]
    for b, ref in enumerate(refs[:-1]):
        refs[-1][pl.ds(b * row_count, row_count), :] = ref[...]


def pair_kernel(own_ref, other_ref, first_ref, *outs):
    row_count = first_ref.shape[0]
    for k, out in enumerate((first_ref,) + outs):
        at = pl.ds(k * row_count, row_count)
        total = own_ref[at, :] + other_ref[at, :].astype(jnp.float32)
        out[...] = total.astype(out.dtype)


def sum_kernel(*refs):
    total = refs[0][...].astype(jnp.float32)
    for ref in refs[1:-1]:
        total += ref[...].astype(jnp.float32)
    refs[-1][...] = total.astype(jnp.bfloat16)


def on_core(kernel, name, outs, ins, scratch=(), limit=8, flops=0):
    return pl.pallas_call(
        kernel,
        out_shape=outs,
        in_specs=ins,
        out_specs=jax.tree.map(lambda out: VMEM, outs),
        scratch_shapes=list(scratch),
        compiler_params=pltpu.CompilerParams(vmem_limit_bytes=limit * 2**20),
        cost_estimate=pl.CostEstimate(flops=flops, bytes_accessed=flops // 4096, transcendentals=0),
        name=name,
    )


def dense_shards(tokens, route_weight, replica, w_gate, w_up, w_down):
    row_count, width = tokens.shape
    hidden_width = w_gate.shape[2]
    peer_count = lax.axis_size("expert")
    half = peer_count // 4
    half_rows = half * row_count
    wide, full = jnp.bfloat16, jnp.float32

    def partner(array, k):
        return lax.ppermute(array, "expert", [(i, i ^ (2 * k)) for i in range(peer_count)])

    def swap(array):
        return lax.ppermute(array, "expert", [(i, i ^ 1) for i in range(peer_count)])

    def shape(rows, dtype, columns=width):
        return jax.ShapeDtypeStruct((rows, columns), dtype)

    def experts(name, blocks, marks=()):
        return on_core(
            functools.partial(expert_kernel, len(blocks)),
            name,
            (shape(half_rows, wide), shape(half_rows, full)),
            [VMEM] * (3 + len(blocks) + len(marks)),
            (
                pltpu.VMEM((2 * half_rows, width), wide),
                pltpu.VMEM((2 * half_rows, LANES), full),
                pltpu.VMEM((2 * half_rows, hidden_width), wide),
            ),
            limit=16,
            flops=10**9,
        )(w_gate, w_up, w_down, *blocks, *marks)

    def pair(own, other, dtype):
        outs = (shape(row_count, dtype),) + (shape(row_count, wide),) * (half - 1)
        return on_core(pair_kernel, "pair", outs, [VMEM] * 2)(own, other)

    def total(name, *terms):
        return on_core(sum_kernel, name, shape(row_count, wide), [VMEM] * len(terms))(*terms)

    packed = on_core(
        pack_kernel,
        "pack",
        shape(row_count, wide, width + LANES),
        [HBM] * 3,
        (
            pltpu.VMEM(replica.shape[::-1], full),
            pltpu.VMEM(replica.shape[::-1], jnp.int32),
            pltpu.SemaphoreType.DMA((3,)),
        ),
        flops=10**10,
    )(*map(in_hbm, (tokens, route_weight.T, replica.T)))
    crossed = partner(packed, half)
    again = on_core(again_kernel, "again", shape(row_count, wide, width + LANES), [VMEM], flops=10**9)(packed)
    order = [1, *range(half - 1, 1, -1)]
    near = [again] + [partner(again, k) for k in order]
    far = [crossed] + [partner(crossed, k) for k in order]
    crossed_other = swap(crossed)
    def join(blocks):
        rows = shape(len(blocks) * row_count, wide, width + LANES)
        return on_core(join_kernel, "join", rows, [VMEM] * len(blocks), flops=10**8)(*blocks)

    near_other = [swap(join(near[: half // 2])), swap(join(near[half // 2 :]))]
    near_away, near_own = experts("near", near_other + near, far[1:])
    far_other = [crossed_other] + [swap(block) for block in far[1:]]
    far_away, far_own = experts("far", far_other + far)
    far_first, *far_sums = pair(far_own, swap(far_away), full)
    near_first, *near_sums = pair(near_own, swap(near_away), full)
    far_back = [partner(block, k) for block, k in zip(far_sums, order)]
    near_back = [partner(block, k) for block, k in zip(near_sums, order)]
    crossing = partner(total("cross", far_first, *far_back), half)
    return total("mix", tokens, near_first, *near_back, crossing)


def routed_shards(tokens, route_weight, replica, w_gate, w_up, w_down):
    row_count, width = tokens.shape
    top_count = replica.shape[1]
    peer_count = lax.axis_size("expert")
    capacity = min(row_count, max(2, 2 * row_count * top_count // peer_count))
    column_count = w_down.shape[2]
    part_index = lax.axis_index("tensor")
    probability = route_weight / jnp.sum(route_weight, axis=1, keepdims=True)
    flat_slot = replica.reshape(-1)
    one_hot = (flat_slot[:, None] == jnp.arange(peer_count, dtype=jnp.int32)[None, :]).astype(
        jnp.int32
    )
    earlier = jnp.cumsum(one_hot, axis=0) - one_hot
    position = jnp.sum(earlier * one_hot, axis=1)
    source_row = jnp.arange(row_count * top_count, dtype=jnp.int32) // top_count
    own_columns = lax.dynamic_slice_in_dim(tokens, part_index * column_count, column_count, 1)
    outgoing = jnp.zeros((peer_count, capacity, width), jnp.bfloat16)
    outgoing = outgoing.at[flat_slot, position].set(tokens[source_row])
    received = lax.all_to_all(outgoing, "expert", split_axis=0, concat_axis=0, tiled=True)
    slot_rows = received.shape[1]
    flat_rows = received.reshape(-1, width)
    gate = jnp.dot(flat_rows, w_gate[0], preferred_element_type=jnp.float32)
    upward = jnp.dot(flat_rows, w_up[0], preferred_element_type=jnp.float32)
    hidden = (jax.nn.silu(gate) * upward).astype(jnp.bfloat16)
    all_hidden = lax.all_gather(hidden, "tensor", axis=1, tiled=True)
    result = jnp.dot(all_hidden, w_down[0], preferred_element_type=jnp.float32).astype(jnp.bfloat16)
    result = result.reshape(peer_count, slot_rows, column_count)
    returned = lax.all_to_all(result, "expert", split_axis=0, concat_axis=0, tiled=True)
    values = returned[flat_slot, position].astype(jnp.float32)
    weighted = values * probability.reshape(-1)[:, None]
    combined = jnp.sum(weighted.reshape(row_count, top_count, column_count), axis=1)
    return (own_columns.astype(jnp.float32) + combined).astype(jnp.bfloat16)


def shards(*arrays):
    tokens, replica, w_gate = arrays[0], arrays[2], arrays[3]
    row_count, top_count = replica.shape
    peer_count = lax.axis_size("expert")
    if (
        lax.axis_size("tensor") == 1
        and peer_count in (16, 32, 64)
        and 2 * top_count >= peer_count
        and row_count % 16 == 0
        and row_count <= LANES
        and tokens.shape[1] % 256 == 0
        and w_gate.shape[2] % 256 == 0
    ):
        return dense_shards(*arrays)
    return routed_shards(*arrays)


def solution(mesh):
    return jax.shard_map(
        shards,
        mesh=mesh,
        in_specs=(
            P(("group", "expert"), None),
            P(("group", "expert"), None),
            P(("group", "expert"), None),
            P("expert", None, "tensor"),
            P("expert", None, "tensor"),
            P("expert", None, "tensor"),
        ),
        out_specs=P(("group", "expert"), "tensor"),
        check_vma=False,
    )
```

```python
import functools
import jax
import jax.numpy as jnp
from jax import lax
from jax.experimental import pallas as pl
from jax.experimental.pallas import tpu as pltpu
from jax.sharding import PartitionSpec as P

LANES = 128
VMEM = pl.BlockSpec(memory_space=pltpu.VMEM)
HBM = pl.BlockSpec(memory_space=pltpu.HBM)


def in_hbm(array):
    return pltpu.with_memory_space_constraint(array, pltpu.HBM)


def pack_kernel(slot_count, token_ref, weight_hbm, replica_hbm, out_ref, weight_ref, replica_ref, sems):
    width = token_ref.shape[1]
    copies = [
        pltpu.make_async_copy(weight_hbm, weight_ref, sems.at[0]),
        pltpu.make_async_copy(replica_hbm, replica_ref, sems.at[1]),
        pltpu.make_async_copy(token_ref, out_ref.at[:, :width], sems.at[2]),
    ]
    for copy in copies:
        copy.start()
    copies[0].wait()
    copies[1].wait()
    weight = weight_ref[...]
    probability = weight / jnp.sum(weight, axis=0, keepdims=True)
    top_count, row_count = weight.shape
    slot = lax.broadcasted_iota(jnp.int32, (slot_count, row_count), 0)
    dense = jnp.zeros((slot_count, row_count), jnp.float32)
    for k in range(top_count):
        dense += jnp.where(replica_ref[k : k + 1, :] == slot, probability[k : k + 1, :], 0.0)
    high = dense.astype(jnp.bfloat16).astype(jnp.float32)
    both = jnp.concatenate([high, dense - high], axis=0).T
    rest = jnp.zeros((row_count, LANES - 2 * slot_count), jnp.float32)
    out_ref[:, width:] = jnp.concatenate([both, rest], axis=1).astype(jnp.bfloat16)
    copies[2].wait()


def expert_kernel(block_count, *refs):
    gate_ref, up_ref, down_ref = refs[:3]
    blocks = refs[3 : 3 + block_count]
    slot = lax.axis_index("expert")
    away_ref, own_ref, rows_ref, share_ref, hidden_ref = refs[-5:]
    width, hidden_width = gate_ref.shape[1:]
    half = own_ref.shape[0]
    first = 0
    for block in blocks:
        row_count = block.shape[0]
        at = pl.ds(first, row_count)
        first += row_count
        rows_ref[at, :] = block[:, :width]
        extra = block[:, width:].astype(jnp.float32)
        lane = lax.broadcasted_iota(jnp.int32, extra.shape, 1)
        chosen = (lane == slot) | (lane == slot + lax.axis_size("expert"))
        share = jnp.sum(jnp.where(chosen, extra, 0.0), axis=1, keepdims=True)
        share_ref[at, :] = jnp.broadcast_to(share, (row_count, LANES))
    rows = rows_ref[...]
    step = 256
    for n in range(0, hidden_width, step):
        gate = jnp.dot(rows, gate_ref[0, :, n : n + step], preferred_element_type=jnp.float32)
        upward = jnp.dot(rows, up_ref[0, :, n : n + step], preferred_element_type=jnp.float32)
        hidden_ref[:, n : n + step] = (gate / (1.0 + jnp.exp(-gate)) * upward).astype(jnp.bfloat16)
    hidden = hidden_ref[...]
    share = share_ref[:, :1]
    for n in range(0, width, step):
        result = jnp.dot(hidden, down_ref[0, :, n : n + step], preferred_element_type=jnp.float32)
        term = result.astype(jnp.bfloat16).astype(jnp.float32) * share
        away_ref[:, n : n + step] = term[:half].astype(jnp.bfloat16)
        own_ref[:, n : n + step] = term[half:]


def again_kernel(source_ref, out_ref):
    out_ref[...] = source_ref[...]


def join_kernel(*refs):
    row_count = refs[0].shape[0]
    for b, ref in enumerate(refs[:-1]):
        refs[-1][pl.ds(b * row_count, row_count), :] = ref[...]


def pair_kernel(own_ref, other_ref, first_ref, *outs):
    row_count = first_ref.shape[0]
    for k, out in enumerate((first_ref,) + outs):
        at = pl.ds(k * row_count, row_count)
        total = own_ref[at, :] + other_ref[at, :].astype(jnp.float32)
        out[...] = total.astype(out.dtype)


def sum_kernel(*refs):
    total = refs[0][...].astype(jnp.float32)
    for ref in refs[1:-1]:
        total += ref[...].astype(jnp.float32)
    refs[-1][...] = total.astype(jnp.bfloat16)


def on_core(kernel, name, outs, ins, scratch=(), limit=8, flops=0):
    return pl.pallas_call(
        kernel,
        out_shape=outs,
        in_specs=ins,
        out_specs=jax.tree.map(lambda out: VMEM, outs),
        scratch_shapes=list(scratch),
        compiler_params=pltpu.CompilerParams(vmem_limit_bytes=limit * 2**20),
        cost_estimate=pl.CostEstimate(flops=flops, bytes_accessed=flops // 4096, transcendentals=0),
        name=name,
    )


def dense_shards(tokens, route_weight, replica, w_gate, w_up, w_down):
    row_count, width = tokens.shape
    hidden_width = w_gate.shape[2]
    peer_count = lax.axis_size("expert")
    half = peer_count // 4
    half_rows = half * row_count
    wide, full = jnp.bfloat16, jnp.float32

    def partner(array, k):
        return lax.ppermute(array, "expert", [(i, i ^ (2 * k)) for i in range(peer_count)])

    def swap(array):
        return lax.ppermute(array, "expert", [(i, i ^ 1) for i in range(peer_count)])

    def shape(rows, dtype, columns=width):
        return jax.ShapeDtypeStruct((rows, columns), dtype)

    def experts(name, blocks, marks=()):
        return on_core(
            functools.partial(expert_kernel, len(blocks)),
            name,
            (shape(half_rows, wide), shape(half_rows, full)),
            [VMEM] * (3 + len(blocks) + len(marks)),
            (
                pltpu.VMEM((2 * half_rows, width), wide),
                pltpu.VMEM((2 * half_rows, LANES), full),
                pltpu.VMEM((2 * half_rows, hidden_width), wide),
            ),
            limit=16,
            flops=10**9,
        )(w_gate, w_up, w_down, *blocks, *marks)

    def pair(own, other, dtype):
        outs = (shape(row_count, dtype),) + (shape(row_count, wide),) * (half - 1)
        return on_core(pair_kernel, "pair", outs, [VMEM] * 2)(own, other)

    def total(name, *terms):
        return on_core(sum_kernel, name, shape(row_count, wide), [VMEM] * len(terms))(*terms)

    packed = on_core(
        functools.partial(pack_kernel, peer_count),
        "pack",
        shape(row_count, wide, width + LANES),
        [HBM] * 3,
        (
            pltpu.VMEM(replica.shape[::-1], full),
            pltpu.VMEM(replica.shape[::-1], jnp.int32),
            pltpu.SemaphoreType.DMA((3,)),
        ),
        flops=10**10,
    )(*map(in_hbm, (tokens, route_weight.T, replica.T)))
    crossed = partner(packed, half)
    again = on_core(again_kernel, "again", shape(row_count, wide, width + LANES), [VMEM], flops=10**10)(packed)
    order = [1, *range(half - 1, 1, -1)]
    near = [again] + [partner(again, k) for k in order]
    far = [crossed] + [partner(crossed, k) for k in order]
    crossed_other = swap(crossed)
    def join(blocks):
        rows = shape(len(blocks) * row_count, wide, width + LANES)
        return on_core(join_kernel, "join", rows, [VMEM] * len(blocks), flops=10**8)(*blocks)

    near_other = [swap(join(near[: half // 2])), swap(join(near[half // 2 :]))]
    near_away, near_own = experts("near", near_other + near, far[1:])
    far_other = [crossed_other] + [swap(block) for block in far[1:]]
    far_away, far_own = experts("far", far_other + far)
    far_first, *far_sums = pair(far_own, swap(far_away), full)
    near_first, *near_sums = pair(near_own, swap(near_away), full)
    far_back = [partner(block, k) for block, k in zip(far_sums, order)]
    near_back = [partner(block, k) for block, k in zip(near_sums, order)]
    crossing = partner(total("cross", far_first, *far_back), half)
    return total("mix", tokens, near_first, *near_back, crossing)


def routed_shards(tokens, route_weight, replica, w_gate, w_up, w_down):
    row_count, width = tokens.shape
    top_count = replica.shape[1]
    peer_count = lax.axis_size("expert")
    capacity = min(row_count, max(2, 2 * row_count * top_count // peer_count))
    column_count = w_down.shape[2]
    part_index = lax.axis_index("tensor")
    probability = route_weight / jnp.sum(route_weight, axis=1, keepdims=True)
    flat_slot = replica.reshape(-1)
    one_hot = (flat_slot[:, None] == jnp.arange(peer_count, dtype=jnp.int32)[None, :]).astype(
        jnp.int32
    )
    earlier = jnp.cumsum(one_hot, axis=0) - one_hot
    position = jnp.sum(earlier * one_hot, axis=1)
    source_row = jnp.arange(row_count * top_count, dtype=jnp.int32) // top_count
    own_columns = lax.dynamic_slice_in_dim(tokens, part_index * column_count, column_count, 1)
    outgoing = jnp.zeros((peer_count, capacity, width), jnp.bfloat16)
    outgoing = outgoing.at[flat_slot, position].set(tokens[source_row])
    received = lax.all_to_all(outgoing, "expert", split_axis=0, concat_axis=0, tiled=True)
    slot_rows = received.shape[1]
    flat_rows = received.reshape(-1, width)
    gate = jnp.dot(flat_rows, w_gate[0], preferred_element_type=jnp.float32)
    upward = jnp.dot(flat_rows, w_up[0], preferred_element_type=jnp.float32)
    hidden = (jax.nn.silu(gate) * upward).astype(jnp.bfloat16)
    all_hidden = lax.all_gather(hidden, "tensor", axis=1, tiled=True)
    result = jnp.dot(all_hidden, w_down[0], preferred_element_type=jnp.float32).astype(jnp.bfloat16)
    result = result.reshape(peer_count, slot_rows, column_count)
    returned = lax.all_to_all(result, "expert", split_axis=0, concat_axis=0, tiled=True)
    values = returned[flat_slot, position].astype(jnp.float32)
    weighted = values * probability.reshape(-1)[:, None]
    combined = jnp.sum(weighted.reshape(row_count, top_count, column_count), axis=1)
    return (own_columns.astype(jnp.float32) + combined).astype(jnp.bfloat16)


def shards(*arrays):
    tokens, replica, w_gate = arrays[0], arrays[2], arrays[3]
    row_count, top_count = replica.shape
    peer_count = lax.axis_size("expert")
    if (
        lax.axis_size("tensor") == 1
        and peer_count in (16, 32, 64)
        and 2 * top_count >= peer_count
        and row_count % 16 == 0
        and row_count <= LANES
        and tokens.shape[1] % 256 == 0
        and w_gate.shape[2] % 256 == 0
    ):
        return dense_shards(*arrays)
    return routed_shards(*arrays)


def solution(mesh):
    return jax.shard_map(
        shards,
        mesh=mesh,
        in_specs=(
            P(("group", "expert"), None),
            P(("group", "expert"), None),
            P(("group", "expert"), None),
            P("expert", None, "tensor"),
            P("expert", None, "tensor"),
            P("expert", None, "tensor"),
        ),
        out_specs=P(("group", "expert"), "tensor"),
        check_vma=False,
    )
```

```python
import functools
import jax
import jax.numpy as jnp
from jax import lax
from jax.experimental import pallas as pl
from jax.experimental.pallas import tpu as pltpu
from jax.sharding import PartitionSpec as P

LANES = 128
VMEM = pl.BlockSpec(memory_space=pltpu.VMEM)
HBM = pl.BlockSpec(memory_space=pltpu.HBM)


def in_hbm(array):
    return pltpu.with_memory_space_constraint(array, pltpu.HBM)


def pack_kernel(slot_count, token_ref, weight_hbm, replica_hbm, out_ref, weight_ref, replica_ref, sems):
    width = token_ref.shape[1]
    copies = [
        pltpu.make_async_copy(weight_hbm, weight_ref, sems.at[0]),
        pltpu.make_async_copy(replica_hbm, replica_ref, sems.at[1]),
    ]
    piece = width // 2
    for p in range(2):
        at = pl.ds(p * piece, piece)
        copies.append(pltpu.make_async_copy(token_ref.at[:, at], out_ref.at[:, at], sems.at[2 + p]))
    for copy in copies:
        copy.start()
    copies[0].wait()
    copies[1].wait()
    weight = weight_ref[...]
    probability = weight / jnp.sum(weight, axis=0, keepdims=True)
    top_count, row_count = weight.shape
    slot = lax.broadcasted_iota(jnp.int32, (slot_count, row_count), 0)
    dense = jnp.zeros((slot_count, row_count), jnp.float32)
    for k in range(top_count):
        dense += jnp.where(replica_ref[k : k + 1, :] == slot, probability[k : k + 1, :], 0.0)
    high = dense.astype(jnp.bfloat16).astype(jnp.float32)
    both = jnp.concatenate([high, dense - high], axis=0).T
    rest = jnp.zeros((row_count, LANES - 2 * slot_count), jnp.float32)
    out_ref[:, width:] = jnp.concatenate([both, rest], axis=1).astype(jnp.bfloat16)
    for copy in copies[2:]:
        copy.wait()


def expert_kernel(block_count, *refs):
    gate_ref, up_ref, down_ref = refs[:3]
    blocks = refs[3 : 3 + block_count]
    slot = lax.axis_index("expert")
    away_ref, own_ref, rows_ref, share_ref, hidden_ref = refs[-5:]
    width, hidden_width = gate_ref.shape[1:]
    half = own_ref.shape[0]
    first = 0
    for block in blocks:
        row_count = block.shape[0]
        at = pl.ds(first, row_count)
        first += row_count
        rows_ref[at, :] = block[:, :width]
        extra = block[:, width:].astype(jnp.float32)
        lane = lax.broadcasted_iota(jnp.int32, extra.shape, 1)
        chosen = (lane == slot) | (lane == slot + lax.axis_size("expert"))
        share = jnp.sum(jnp.where(chosen, extra, 0.0), axis=1, keepdims=True)
        share_ref[at, :] = jnp.broadcast_to(share, (row_count, LANES))
    rows = rows_ref[...]
    step = 256
    for n in range(0, hidden_width, step):
        gate = jnp.dot(rows, gate_ref[0, :, n : n + step], preferred_element_type=jnp.float32)
        upward = jnp.dot(rows, up_ref[0, :, n : n + step], preferred_element_type=jnp.float32)
        hidden_ref[:, n : n + step] = (gate / (1.0 + jnp.exp(-gate)) * upward).astype(jnp.bfloat16)
    hidden = hidden_ref[...]
    share = share_ref[:, :1]
    for n in range(0, width, step):
        result = jnp.dot(hidden, down_ref[0, :, n : n + step], preferred_element_type=jnp.float32)
        term = result.astype(jnp.bfloat16).astype(jnp.float32) * share
        away_ref[:, n : n + step] = term[:half].astype(jnp.bfloat16)
        own_ref[:, n : n + step] = term[half:]


def again_kernel(source_ref, out_ref):
    out_ref[...] = source_ref[...]


def join_kernel(*refs):
    row_count = refs[0].shape[0]
    for b, ref in enumerate(refs[:-1]):
        refs[-1][pl.ds(b * row_count, row_count), :] = ref[...]


def pair_kernel(own_ref, other_ref, first_ref, *outs):
    row_count = first_ref.shape[0]
    for k, out in enumerate((first_ref,) + outs):
        at = pl.ds(k * row_count, row_count)
        total = own_ref[at, :] + other_ref[at, :].astype(jnp.float32)
        out[...] = total.astype(out.dtype)


def sum_kernel(*refs):
    total = refs[0][...].astype(jnp.float32)
    for ref in refs[1:-1]:
        total += ref[...].astype(jnp.float32)
    refs[-1][...] = total.astype(jnp.bfloat16)


def on_core(kernel, name, outs, ins, scratch=(), limit=8, flops=0):
    return pl.pallas_call(
        kernel,
        out_shape=outs,
        in_specs=ins,
        out_specs=jax.tree.map(lambda out: VMEM, outs),
        scratch_shapes=list(scratch),
        compiler_params=pltpu.CompilerParams(vmem_limit_bytes=limit * 2**20),
        cost_estimate=pl.CostEstimate(flops=flops, bytes_accessed=flops // 4096, transcendentals=0),
        name=name,
    )


def dense_shards(tokens, route_weight, replica, w_gate, w_up, w_down):
    row_count, width = tokens.shape
    hidden_width = w_gate.shape[2]
    peer_count = lax.axis_size("expert")
    half = peer_count // 4
    half_rows = half * row_count
    wide, full = jnp.bfloat16, jnp.float32

    def partner(array, k):
        return lax.ppermute(array, "expert", [(i, i ^ (2 * k)) for i in range(peer_count)])

    def swap(array):
        return lax.ppermute(array, "expert", [(i, i ^ 1) for i in range(peer_count)])

    def shape(rows, dtype, columns=width):
        return jax.ShapeDtypeStruct((rows, columns), dtype)

    def experts(name, blocks, marks=()):
        return on_core(
            functools.partial(expert_kernel, len(blocks)),
            name,
            (shape(half_rows, wide), shape(half_rows, full)),
            [VMEM] * (3 + len(blocks) + len(marks)),
            (
                pltpu.VMEM((2 * half_rows, width), wide),
                pltpu.VMEM((2 * half_rows, LANES), full),
                pltpu.VMEM((2 * half_rows, hidden_width), wide),
            ),
            limit=16,
            flops=10**9,
        )(w_gate, w_up, w_down, *blocks, *marks)

    def pair(own, other, dtype):
        outs = (shape(row_count, dtype),) + (shape(row_count, wide),) * (half - 1)
        return on_core(pair_kernel, "pair", outs, [VMEM] * 2)(own, other)

    def total(name, *terms):
        return on_core(sum_kernel, name, shape(row_count, wide), [VMEM] * len(terms))(*terms)

    packed = on_core(
        functools.partial(pack_kernel, peer_count),
        "pack",
        shape(row_count, wide, width + LANES),
        [HBM] * 3,
        (
            pltpu.VMEM(replica.shape[::-1], full),
            pltpu.VMEM(replica.shape[::-1], jnp.int32),
            pltpu.SemaphoreType.DMA((4,)),
        ),
        flops=10**10,
    )(*map(in_hbm, (tokens, route_weight.T, replica.T)))
    crossed = partner(packed, half)
    again = on_core(again_kernel, "again", shape(row_count, wide, width + LANES), [VMEM], flops=10**10)(packed)
    order = [1, *range(half - 1, 1, -1)]
    near = [again] + [partner(again, k) for k in order]
    far = [crossed] + [partner(crossed, k) for k in order]
    crossed_other = swap(crossed)
    def join(blocks):
        rows = shape(len(blocks) * row_count, wide, width + LANES)
        return on_core(join_kernel, "join", rows, [VMEM] * len(blocks), flops=10**8)(*blocks)

    near_other = [swap(join(near[: half // 2])), swap(join(near[half // 2 :]))]
    near_away, near_own = experts("near", near_other + near, far[1:])
    far_other = [crossed_other] + [swap(block) for block in far[1:]]
    far_away, far_own = experts("far", far_other + far)
    far_first, *far_sums = pair(far_own, swap(far_away), full)
    near_first, *near_sums = pair(near_own, swap(near_away), full)
    far_back = [partner(block, k) for block, k in zip(far_sums, order)]
    near_back = [partner(block, k) for block, k in zip(near_sums, order)]
    crossing = partner(total("cross", far_first, *far_back), half)
    return total("mix", tokens, near_first, *near_back, crossing)


def routed_shards(tokens, route_weight, replica, w_gate, w_up, w_down):
    row_count, width = tokens.shape
    top_count = replica.shape[1]
    peer_count = lax.axis_size("expert")
    capacity = min(row_count, max(2, 2 * row_count * top_count // peer_count))
    column_count = w_down.shape[2]
    part_index = lax.axis_index("tensor")
    probability = route_weight / jnp.sum(route_weight, axis=1, keepdims=True)
    flat_slot = replica.reshape(-1)
    one_hot = (flat_slot[:, None] == jnp.arange(peer_count, dtype=jnp.int32)[None, :]).astype(
        jnp.int32
    )
    earlier = jnp.cumsum(one_hot, axis=0) - one_hot
    position = jnp.sum(earlier * one_hot, axis=1)
    source_row = jnp.arange(row_count * top_count, dtype=jnp.int32) // top_count
    own_columns = lax.dynamic_slice_in_dim(tokens, part_index * column_count, column_count, 1)
    outgoing = jnp.zeros((peer_count, capacity, width), jnp.bfloat16)
    outgoing = outgoing.at[flat_slot, position].set(tokens[source_row])
    received = lax.all_to_all(outgoing, "expert", split_axis=0, concat_axis=0, tiled=True)
    slot_rows = received.shape[1]
    flat_rows = received.reshape(-1, width)
    gate = jnp.dot(flat_rows, w_gate[0], preferred_element_type=jnp.float32)
    upward = jnp.dot(flat_rows, w_up[0], preferred_element_type=jnp.float32)
    hidden = (jax.nn.silu(gate) * upward).astype(jnp.bfloat16)
    all_hidden = lax.all_gather(hidden, "tensor", axis=1, tiled=True)
    result = jnp.dot(all_hidden, w_down[0], preferred_element_type=jnp.float32).astype(jnp.bfloat16)
    result = result.reshape(peer_count, slot_rows, column_count)
    returned = lax.all_to_all(result, "expert", split_axis=0, concat_axis=0, tiled=True)
    values = returned[flat_slot, position].astype(jnp.float32)
    weighted = values * probability.reshape(-1)[:, None]
    combined = jnp.sum(weighted.reshape(row_count, top_count, column_count), axis=1)
    return (own_columns.astype(jnp.float32) + combined).astype(jnp.bfloat16)


def shards(*arrays):
    tokens, replica, w_gate = arrays[0], arrays[2], arrays[3]
    row_count, top_count = replica.shape
    peer_count = lax.axis_size("expert")
    if (
        lax.axis_size("tensor") == 1
        and peer_count in (16, 32, 64)
        and 2 * top_count >= peer_count
        and row_count % 16 == 0
        and row_count <= LANES
        and tokens.shape[1] % 256 == 0
        and w_gate.shape[2] % 256 == 0
    ):
        return dense_shards(*arrays)
    return routed_shards(*arrays)


def solution(mesh):
    return jax.shard_map(
        shards,
        mesh=mesh,
        in_specs=(
            P(("group", "expert"), None),
            P(("group", "expert"), None),
            P(("group", "expert"), None),
            P("expert", None, "tensor"),
            P("expert", None, "tensor"),
            P("expert", None, "tensor"),
        ),
        out_specs=P(("group", "expert"), "tensor"),
        check_vma=False,
    )
```

```python
import functools
import jax
import jax.numpy as jnp
from jax import lax
from jax.experimental import pallas as pl
from jax.experimental.pallas import tpu as pltpu
from jax.sharding import PartitionSpec as P

LANES = 128
VMEM = pl.BlockSpec(memory_space=pltpu.VMEM)
HBM = pl.BlockSpec(memory_space=pltpu.HBM)


def in_hbm(array):
    return pltpu.with_memory_space_constraint(array, pltpu.HBM)


def pack_kernel(slot_count, token_ref, weight_hbm, replica_hbm, out_ref, weight_ref, replica_ref, sems):
    width = token_ref.shape[1]
    copies = [
        pltpu.make_async_copy(weight_hbm, weight_ref, sems.at[0]),
        pltpu.make_async_copy(replica_hbm, replica_ref, sems.at[1]),
    ]
    piece = width // 2
    for p in range(2):
        at = pl.ds(p * piece, piece)
        copies.append(pltpu.make_async_copy(token_ref.at[:, at], out_ref.at[:, at], sems.at[2 + p]))
    for copy in copies:
        copy.start()
    copies[0].wait()
    copies[1].wait()
    weight = weight_ref[...]
    probability = weight / jnp.sum(weight, axis=0, keepdims=True)
    top_count, row_count = weight.shape
    slot = lax.broadcasted_iota(jnp.int32, (slot_count, row_count), 0)
    dense = jnp.zeros((slot_count, row_count), jnp.float32)
    for k in range(top_count):
        dense += jnp.where(replica_ref[k : k + 1, :] == slot, probability[k : k + 1, :], 0.0)
    high = dense.astype(jnp.bfloat16).astype(jnp.float32)
    both = jnp.concatenate([high, dense - high], axis=0).T
    rest = jnp.zeros((row_count, LANES - 2 * slot_count), jnp.float32)
    out_ref[:, width:] = jnp.concatenate([both, rest], axis=1).astype(jnp.bfloat16)
    for copy in copies[2:]:
        copy.wait()


def expert_kernel(block_count, *refs):
    gate_ref, up_ref, down_ref = refs[:3]
    blocks = refs[3 : 3 + block_count]
    slot = lax.axis_index("expert")
    away_ref, own_ref, rows_ref, share_ref, hidden_ref = refs[-5:]
    width, hidden_width = gate_ref.shape[1:]
    half = own_ref.shape[0]
    first = 0
    for block in blocks:
        row_count = block.shape[0]
        at = pl.ds(first, row_count)
        first += row_count
        rows_ref[at, :] = block[:, :width]
        extra = block[:, width:].astype(jnp.float32)
        lane = lax.broadcasted_iota(jnp.int32, extra.shape, 1)
        chosen = (lane == slot) | (lane == slot + lax.axis_size("expert"))
        share = jnp.sum(jnp.where(chosen, extra, 0.0), axis=1, keepdims=True)
        share_ref[at, :] = jnp.broadcast_to(share, (row_count, LANES))
    rows = rows_ref[...]
    step = 256
    for n in range(0, hidden_width, step):
        gate = jnp.dot(rows, gate_ref[0, :, n : n + step], preferred_element_type=jnp.float32)
        upward = jnp.dot(rows, up_ref[0, :, n : n + step], preferred_element_type=jnp.float32)
        hidden_ref[:, n : n + step] = (gate / (1.0 + jnp.exp(-gate)) * upward).astype(jnp.bfloat16)
    hidden = hidden_ref[...]
    share = share_ref[:, :1]
    for n in range(0, width, step):
        result = jnp.dot(hidden, down_ref[0, :, n : n + step], preferred_element_type=jnp.float32)
        term = result.astype(jnp.bfloat16).astype(jnp.float32) * share
        away_ref[:, n : n + step] = term[:half].astype(jnp.bfloat16)
        own_ref[:, n : n + step] = term[half:]


def again_kernel(source_ref, out_ref):
    out_ref[...] = source_ref[...]


def join_kernel(*refs):
    row_count = refs[0].shape[0]
    for b, ref in enumerate(refs[:-1]):
        refs[-1][pl.ds(b * row_count, row_count), :] = ref[...]


def pair_kernel(own_ref, other_ref, first_ref, *outs):
    row_count = first_ref.shape[0]
    for k, out in enumerate((first_ref,) + outs):
        at = pl.ds(k * row_count, row_count)
        total = own_ref[at, :] + other_ref[at, :].astype(jnp.float32)
        out[...] = total.astype(out.dtype)


def sum_kernel(*refs):
    total = refs[0][...].astype(jnp.float32)
    for ref in refs[1:-1]:
        total += ref[...].astype(jnp.float32)
    refs[-1][...] = total.astype(jnp.bfloat16)


def mix_kernel(*refs):
    out_hbm, total_ref, sems = refs[-3:]
    piece = total_ref.shape[1] // 2
    copies = []
    for p in range(2):
        at = pl.ds(p * piece, piece)
        total = refs[0][:, at].astype(jnp.float32)
        for ref in refs[1:-3]:
            total += ref[:, at].astype(jnp.float32)
        total_ref[:, at] = total.astype(jnp.bfloat16)
        copies.append(pltpu.make_async_copy(total_ref.at[:, at], out_hbm.at[:, at], sems.at[p]))
        copies[-1].start()
    for copy in copies:
        copy.wait()


def on_core(kernel, name, outs, ins, scratch=(), limit=8, flops=0):
    return pl.pallas_call(
        kernel,
        out_shape=outs,
        in_specs=ins,
        out_specs=jax.tree.map(lambda out: VMEM, outs),
        scratch_shapes=list(scratch),
        compiler_params=pltpu.CompilerParams(vmem_limit_bytes=limit * 2**20),
        cost_estimate=pl.CostEstimate(flops=flops, bytes_accessed=flops // 4096, transcendentals=0),
        name=name,
    )


def dense_shards(tokens, route_weight, replica, w_gate, w_up, w_down):
    row_count, width = tokens.shape
    hidden_width = w_gate.shape[2]
    peer_count = lax.axis_size("expert")
    half = peer_count // 4
    half_rows = half * row_count
    wide, full = jnp.bfloat16, jnp.float32

    def partner(array, k):
        return lax.ppermute(array, "expert", [(i, i ^ (2 * k)) for i in range(peer_count)])

    def swap(array):
        return lax.ppermute(array, "expert", [(i, i ^ 1) for i in range(peer_count)])

    def shape(rows, dtype, columns=width):
        return jax.ShapeDtypeStruct((rows, columns), dtype)

    def experts(name, blocks, marks=()):
        return on_core(
            functools.partial(expert_kernel, len(blocks)),
            name,
            (shape(half_rows, wide), shape(half_rows, full)),
            [VMEM] * (3 + len(blocks) + len(marks)),
            (
                pltpu.VMEM((2 * half_rows, width), wide),
                pltpu.VMEM((2 * half_rows, LANES), full),
                pltpu.VMEM((2 * half_rows, hidden_width), wide),
            ),
            limit=16,
            flops=10**9,
        )(w_gate, w_up, w_down, *blocks, *marks)

    def pair(own, other, dtype):
        outs = (shape(row_count, dtype),) + (shape(row_count, wide),) * (half - 1)
        return on_core(pair_kernel, "pair", outs, [VMEM] * 2)(own, other)

    def total(name, *terms):
        return on_core(sum_kernel, name, shape(row_count, wide), [VMEM] * len(terms))(*terms)

    packed = on_core(
        functools.partial(pack_kernel, peer_count),
        "pack",
        shape(row_count, wide, width + LANES),
        [HBM] * 3,
        (
            pltpu.VMEM(replica.shape[::-1], full),
            pltpu.VMEM(replica.shape[::-1], jnp.int32),
            pltpu.SemaphoreType.DMA((4,)),
        ),
        flops=10**10,
    )(*map(in_hbm, (tokens, route_weight.T, replica.T)))
    crossed = partner(packed, half)
    again = on_core(again_kernel, "again", shape(row_count, wide, width + LANES), [VMEM], flops=10**10)(packed)
    order = [1, *range(half - 1, 1, -1)]
    near = [again] + [partner(again, k) for k in order]
    far = [crossed] + [partner(crossed, k) for k in order]
    crossed_other = swap(crossed)
    def join(blocks):
        rows = shape(len(blocks) * row_count, wide, width + LANES)
        return on_core(join_kernel, "join", rows, [VMEM] * len(blocks), flops=10**8)(*blocks)

    near_other = [swap(join(near[: half // 2])), swap(join(near[half // 2 :]))]
    near_away, near_own = experts("near", near_other + near, far[1:])
    far_other = [crossed_other] + [swap(block) for block in far[1:]]
    far_away, far_own = experts("far", far_other + far)
    far_first, *far_sums = pair(far_own, swap(far_away), full)
    near_first, *near_sums = pair(near_own, swap(near_away), full)
    far_back = [partner(block, k) for block, k in zip(far_sums, order)]
    near_back = [partner(block, k) for block, k in zip(near_sums, order)]
    crossing = partner(total("cross", far_first, *far_back), half)
    terms = (tokens, near_first, *near_back, crossing)
    return pl.pallas_call(
        mix_kernel,
        out_shape=shape(row_count, wide),
        in_specs=[VMEM] * len(terms),
        out_specs=HBM,
        scratch_shapes=[pltpu.VMEM((row_count, width), wide), pltpu.SemaphoreType.DMA((2,))],
        compiler_params=pltpu.CompilerParams(vmem_limit_bytes=8 * 2**20),
        name="mix",
    )(*terms)


def routed_shards(tokens, route_weight, replica, w_gate, w_up, w_down):
    row_count, width = tokens.shape
    top_count = replica.shape[1]
    peer_count = lax.axis_size("expert")
    capacity = min(row_count, max(2, 2 * row_count * top_count // peer_count))
    column_count = w_down.shape[2]
    part_index = lax.axis_index("tensor")
    probability = route_weight / jnp.sum(route_weight, axis=1, keepdims=True)
    flat_slot = replica.reshape(-1)
    one_hot = (flat_slot[:, None] == jnp.arange(peer_count, dtype=jnp.int32)[None, :]).astype(
        jnp.int32
    )
    earlier = jnp.cumsum(one_hot, axis=0) - one_hot
    position = jnp.sum(earlier * one_hot, axis=1)
    source_row = jnp.arange(row_count * top_count, dtype=jnp.int32) // top_count
    own_columns = lax.dynamic_slice_in_dim(tokens, part_index * column_count, column_count, 1)
    outgoing = jnp.zeros((peer_count, capacity, width), jnp.bfloat16)
    outgoing = outgoing.at[flat_slot, position].set(tokens[source_row])
    received = lax.all_to_all(outgoing, "expert", split_axis=0, concat_axis=0, tiled=True)
    slot_rows = received.shape[1]
    flat_rows = received.reshape(-1, width)
    gate = jnp.dot(flat_rows, w_gate[0], preferred_element_type=jnp.float32)
    upward = jnp.dot(flat_rows, w_up[0], preferred_element_type=jnp.float32)
    hidden = (jax.nn.silu(gate) * upward).astype(jnp.bfloat16)
    all_hidden = lax.all_gather(hidden, "tensor", axis=1, tiled=True)
    result = jnp.dot(all_hidden, w_down[0], preferred_element_type=jnp.float32).astype(jnp.bfloat16)
    result = result.reshape(peer_count, slot_rows, column_count)
    returned = lax.all_to_all(result, "expert", split_axis=0, concat_axis=0, tiled=True)
    values = returned[flat_slot, position].astype(jnp.float32)
    weighted = values * probability.reshape(-1)[:, None]
    combined = jnp.sum(weighted.reshape(row_count, top_count, column_count), axis=1)
    return (own_columns.astype(jnp.float32) + combined).astype(jnp.bfloat16)


def shards(*arrays):
    tokens, replica, w_gate = arrays[0], arrays[2], arrays[3]
    row_count, top_count = replica.shape
    peer_count = lax.axis_size("expert")
    if (
        lax.axis_size("tensor") == 1
        and peer_count in (16, 32, 64)
        and 2 * top_count >= peer_count
        and row_count % 16 == 0
        and row_count <= LANES
        and tokens.shape[1] % 256 == 0
        and w_gate.shape[2] % 256 == 0
    ):
        return dense_shards(*arrays)
    return routed_shards(*arrays)


def solution(mesh):
    return jax.shard_map(
        shards,
        mesh=mesh,
        in_specs=(
            P(("group", "expert"), None),
            P(("group", "expert"), None),
            P(("group", "expert"), None),
            P("expert", None, "tensor"),
            P("expert", None, "tensor"),
            P("expert", None, "tensor"),
        ),
        out_specs=P(("group", "expert"), "tensor"),
        check_vma=False,
    )
```
